512 devices in a mesh: section: 8 (over y, x_lo), lon: 64 (over x_hi, z, core).
Axes of the slice: x: 4 (x_hi: 2, x_lo: 2; x = x_hi * 2 + x_lo), y: 4, z: 16, core: 2. Of those that a mesh axis runs over, the one named last changes fastest.
Arguments:
- inputs: bfloat16 [3, 2, 12, 768, 512], P(None, None, None, 'lon'), may hold values from -6 to 6
- norm_gain: float32 [8, 512], P('section'), may hold values from 0.1 to 1.9
- w_qkv: bfloat16 [8, 512, 1536], P('section'), may hold values from -1.3258252 to 1.3258252
- w_out: bfloat16 [8, 512, 512], P('section'), may hold values from -0.25 to 0.25
- w_head: bfloat16 [512, 1024], P(None, 'section'), may hold values from -0.25 to 0.25
Outputs:
- decoded: bfloat16 [3, 2, 12, 768, 1024], P(None, None, None, 'lon', 'section')
The draws below stay inside these ranges and needn't reach their ends.
All inputs are finite; a program needn't handle non-finite values.
Results may differ from the reference program's by a relative error of at most 0.019.
Values may be sent and summed in bfloat16 or wider, within the bound.
A program may use at most 64 MiB of HBM per device.

```python
import jax
import jax.numpy as jnp
from jax import lax

D = 512
HEADS = 8
OUTC = 1024
Z_LEV = 2
WIN_LAT = 6
WIN_LON = 12
SHIFT = 6
LAT = 12
MICRO = 3
LON = 768
SECTIONS = 8


def draw_w_qkv(key, part):
    key = jax.random.fold_in(key, 7)
    base = jnp.clip(jax.random.normal(key, (SECTIONS, D, 3 * D), jnp.float32), -5.0, 5.0) * D ** (-0.5)
    return base.astype(jnp.bfloat16)


def shard_levels(rng, shape, split, smallest, top_value):
    level, own = 1.0, jax.random.fold_in(rng, 6)
    for position, shards_of in split:
        steps = jnp.exp(jax.random.uniform(jax.random.fold_in(own, position), (shards_of,), jnp.float32, smallest / len(split), top_value / len(split)))
        level = level * jnp.repeat(steps, shape[position] // shards_of).reshape([-1 if axis == position else 1 for axis in range(len(shape))])
    return level


def normal_values(key, extent, deviation, most, cuts=(), held_as=jnp.bfloat16):
    drawn = deviation * jax.random.normal(key, extent, jnp.float32)
    if cuts:
        drawn = drawn * shard_levels(key, extent, cuts, -0.22, 0.18)
    return jnp.clip(drawn, -most, most).astype(held_as)


def setup_inputs(seed: int = 0) -> dict:
    key_of = jax.random.split(jax.random.key(seed), 6)
    return {
        "inputs": normal_values(key_of[0], (MICRO, Z_LEV, LAT, LON, D), 1.0, 6.0, ((3, 64),)),
        "norm_gain": jnp.clip(1.0 + 0.18 * jax.random.normal(key_of[1], (SECTIONS, D), jnp.float32), 0.1, 1.9),
        "w_qkv": draw_w_qkv(jax.random.fold_in(key_of[5], 71), 0),
        "w_out": normal_values(key_of[3], (SECTIONS, D, D), D ** -0.5, 0.25, ((0, 8),)),
        "w_head": normal_values(key_of[4], (D, OUTC), D ** -0.5, 0.25, ((1, 8),)),
    }


EPS = 1e-05

def normalize(field, gain):
    values = field.astype(jnp.float32)
    mean = lax.optimization_barrier(jnp.mean(values, axis=-1, keepdims=True))
    centred = values - mean
    spread = lax.optimization_barrier(jnp.mean(centred * centred, axis=-1, keepdims=True))
    return (centred * lax.rsqrt(spread + EPS) * gain).astype(jnp.bfloat16)

def to_windows(field):
    levels, lat, lon, width = field.shape
    blocks = field.reshape(levels, lat // WIN_LAT, WIN_LAT, lon // WIN_LON, WIN_LON, width)
    blocks = blocks.transpose(1, 3, 0, 2, 4, 5)
    return blocks.reshape(-1, levels * WIN_LAT * WIN_LON, width)

def from_windows(blocks, levels, lat, lon):
    width = blocks.shape[-1]
    blocks = blocks.reshape(lat // WIN_LAT, lon // WIN_LON, levels, WIN_LAT, WIN_LON, width)
    return blocks.transpose(2, 0, 3, 1, 4, 5).reshape(levels, lat, lon, width)

def attend(field, gain, w_qkv, w_out):
    levels, lat, lon, width = field.shape
    normed = normalize(field, gain)
    blocks = to_windows(normed)
    count_win, count, _ = blocks.shape
    qkv = jnp.dot(blocks.reshape(-1, width), w_qkv, preferred_element_type=jnp.float32).astype(jnp.bfloat16)
    qkv = qkv.reshape(count_win, count, 3, HEADS, width // HEADS)
    query = qkv[:, :, 0].astype(jnp.float32)
    keys = qkv[:, :, 1].astype(jnp.float32)
    values = qkv[:, :, 2].astype(jnp.float32)
    scores = jnp.einsum('wqhe,wkhe->whqk', query, keys) * (width // HEADS) ** (-0.5)
    scores = scores - lax.optimization_barrier(jnp.max(scores, axis=-1, keepdims=True))
    weights = jnp.exp(scores)
    probs = (weights / lax.optimization_barrier(jnp.sum(weights, axis=-1, keepdims=True))).astype(jnp.bfloat16)
    mixed = jnp.einsum('whqk,wkhe->wqhe', probs.astype(jnp.float32), values).astype(jnp.bfloat16)
    proj = jnp.dot(mixed.reshape(-1, width), w_out, preferred_element_type=jnp.float32)
    back = from_windows(proj.reshape(count_win, count, width), levels, lat, lon)
    return (field.astype(jnp.float32) + back).astype(jnp.bfloat16)

def reference(inputs, norm_gain, w_qkv, w_out, w_head):
    sections = norm_gain.shape[0]
    first_dec = sections // 2 + sections // 8
    results = []
    for micro in range(MICRO):
        field = inputs[micro]
        saved = {}
        for section in range(sections):
            if section >= first_dec:
                field = (field.astype(jnp.float32) + saved[section - first_dec].astype(jnp.float32)).astype(jnp.bfloat16)
            if section % 2 == 1:
                field = jnp.roll(field, -SHIFT, axis=2)
            field = attend(field, norm_gain[section], w_qkv[section], w_out[section])
            if section % 2 == 1:
                field = jnp.roll(field, SHIFT, axis=2)
            saved[section] = field
        levels, lat, lon, width = field.shape
        head = jnp.dot(field.reshape(-1, width), w_head, preferred_element_type=jnp.float32)
        results.append(head.astype(jnp.bfloat16).reshape(levels, lat, lon, -1))
    return jnp.stack(results)
```

```python
import functools

import jax
import jax.numpy as jnp
from jax import lax
from jax.experimental import pallas as pl
from jax.experimental.pallas import tpu as pltpu
from jax.sharding import PartitionSpec as P

MESH = pl.DeviceIdType.MESH
F32, BF16 = jnp.float32, jnp.bfloat16
HEADS = 8
HALF = 72
PAD = 80
WIN = 2 * HALF
EPS = 1e-05
LAYERS = 8
SKIP = 5
LANES = 128


def dot(a, b):
    return jnp.dot(a, b, preferred_element_type=F32)


def dot_t(a, b):
    return lax.dot_general(a, b, (((1,), (1,)), ((), ())), preferred_element_type=F32)


def normalize(x, gain):
    mean = jnp.mean(x, axis=-1, keepdims=True)
    centred = x - mean
    spread = jnp.mean(centred * centred, axis=-1, keepdims=True)
    return (centred * lax.rsqrt(spread + EPS) * gain).astype(BF16)


def attend(query, kv, width):
    rows = query.shape[0]
    low = lax.broadcasted_iota(jnp.int32, (rows, LANES), 1) < LANES // 2
    mixed = []
    for pair in range(width // LANES):
        cols = slice(pair * LANES, (pair + 1) * LANES)
        q = query[:, cols]
        both = jnp.concatenate([jnp.where(low, q, 0.0), jnp.where(low, 0.0, q)], 0).astype(BF16)
        scores = dot_t(both, kv[:, cols])
        top = jnp.max(scores, axis=-1, keepdims=True)
        weights = jnp.exp2(scores - top).astype(BF16)
        values = kv[:, width + pair * LANES : width + (pair + 1) * LANES]
        summed = dot(weights, jnp.concatenate([values, jnp.ones_like(values)], 1))
        summed = summed[:, :LANES] / summed[:, LANES:]
        mixed.append(jnp.where(low, summed[:rows], summed[rows:]))
    return jnp.concatenate(mixed, 1).astype(BF16)


def swizzled(lon, lons):
    high, low = lon // (lons // 2), lax.rem(lon, 2)
    swapped = high + low - 2 * high * low
    return lax.rem(lon, lons // 2) + swapped * (lons // 2)


def kernel(micro, x_ref, gain_ref, wqkv_ref, wout_ref, whead_ref, out_ref,
           xin, gain, wqkv, wout, whead, xs, kv, arrived, skips, sent, outs, outs_in, halves, joined,
           load_sem, arrive_sem, send_sem, skip_sem, skipsend_sem, head_sem, headsend_sem, out_sem, outsend_sem):
    sections, lons = lax.axis_size("section"), lax.axis_size("lon")
    sec, lon = lax.axis_index("section"), lax.axis_index("lon")
    odd = lax.rem(sec, 2)
    width = wout_ref.shape[-1]
    streams = 2 * micro
    last = sections - 1
    mine = jnp.where(odd == 1, swizzled(lon, lons), lon)

    def holder(section, block):
        block = lax.rem(block + lons, lons)
        return section, jnp.where(lax.rem(section, 2) == 1, swizzled(block, lons), block)

    def target(half, to):
        return holder(to, mine + half - 1 + odd)

    loads = [
        pltpu.make_async_copy(gain_ref, gain, load_sem.at[0]),
        pltpu.make_async_copy(wqkv_ref.at[0], wqkv, load_sem.at[1]),
        pltpu.make_async_copy(wout_ref.at[0], wout, load_sem.at[2]),
        pltpu.make_async_copy(whead_ref, whead.at[sec], load_sem.at[3]),
    ]
    for load in loads:
        load.start()
    load_x = pltpu.make_async_copy(x_ref, xin, load_sem.at[4])
    pl.when(sec == 0)(load_x.start)

    barrier = pltpu.get_barrier_semaphore()

    def greet(where):
        pl.semaphore_signal(barrier, inc=1, device_id=where, device_id_type=MESH)

    def greet_sources(behind):
        before = sec - behind
        was_odd = lax.rem(before, 2)
        for half in range(2):
            greet(holder(before, mine - (half - 1 + was_odd)))

    pl.when(sec > 0)(lambda: greet_sources(1))
    pl.when(sec >= SKIP)(lambda: greet_sources(SKIP))

    @pl.when(sec == last)
    def _():
        for c in range(last):
            greet((c, lon))

    def out_source(half):
        return holder(last, lon - half)

    for half in range(2):
        where = out_source(half)
        here = jnp.logical_and(sec == last, where[1] == lon)
        pl.when(jnp.logical_not(here))(functools.partial(greet, where))

    itself = jnp.logical_and(sec == last, mine == lon)
    itself_next = jnp.logical_and(sec == last, lax.rem(mine + 1, lons) == lon)
    count = jnp.where(sec < last, 3, 2 * sections)
    count = count + jnp.where(sec < LAYERS - SKIP, 2, 0)
    count = count - jnp.where(itself, 1, 0) - jnp.where(itself_next, 1, 0)
    pl.semaphore_wait(barrier, count)

    head_copy = pltpu.make_async_remote_copy(
        src_ref=whead.at[sec], dst_ref=whead.at[sec], send_sem=headsend_sem, recv_sem=head_sem.at[sec],
        device_id=(last, lon), device_id_type=MESH)
    for load in loads:
        load.wait()

    pl.when(jnp.logical_and(sec >= 3, sec < last))(head_copy.start)
    pl.when(sec == 0)(load_x.wait)

    def step_copy(stream, half):
        return pltpu.make_async_remote_copy(
            src_ref=sent.at[stream, half], dst_ref=arrived.at[stream, 1 - half],
            send_sem=send_sem.at[stream, half], recv_sem=arrive_sem.at[stream, 1 - half],
            device_id=target(half, jnp.minimum(sec + 1, last)), device_id_type=MESH)

    def skip_copy(stream, half):
        return pltpu.make_async_remote_copy(
            src_ref=sent.at[stream, half], dst_ref=skips.at[stream, 1 - half],
            send_sem=skipsend_sem.at[stream, half], recv_sem=skip_sem.at[stream, 1 - half],
            device_id=target(half, jnp.minimum(sec + SKIP, last)), device_id_type=MESH)

    def out_copy(stream, half, c):
        return pltpu.make_async_remote_copy(
            src_ref=outs.at[stream, half, c], dst_ref=outs_in.at[stream, 1 - half],
            send_sem=outsend_sem.at[stream, half, c], recv_sem=out_sem.at[stream, 1 - half],
            device_id=(c, lax.rem(mine + half, lons)), device_id_type=MESH)

    def out_local(stream, half, c):
        return pltpu.make_async_copy(outs.at[stream, half, c], outs_in.at[stream, 1 - half], out_sem.at[stream, 1 - half])

    stays = (itself, itself_next)

    def step(stream, carry):
        @pl.when(sec == 0)
        def _():
            m, lat = stream // 2, lax.rem(stream, 2)
            for level in range(2):
                for a in range(6):
                    block = xin[m, level, lat * 6 + a].astype(F32)
                    at = (level * 6 + a) * 6
                    xs[at : at + 6] = block[:6]
                    xs[HALF + at : HALF + at + 6] = block[6:]

        @pl.when(sec > 0)
        def _():
            for half in range(2):
                step_copy(stream, 1 - half).wait_recv()

        @pl.when(jnp.logical_and(sec > 0, sec < SKIP))
        def _():
            for half in range(2):
                xs[half * HALF : (half + 1) * HALF] = arrived[stream, half].astype(F32)[:HALF]

        @pl.when(sec >= SKIP)
        def _():
            for half in range(2):
                skip_copy(stream, 1 - half).wait_recv()
                joined_up = arrived[stream, half].astype(F32) + skips[stream, half].astype(F32)
                xs[half * HALF : (half + 1) * HALF] = joined_up.astype(BF16).astype(F32)[:HALF]

        x = xs[...]
        normed = normalize(x, gain[...])
        query = dot(normed, wqkv[:, :width]) * ((width // HEADS) ** -0.5 * 1.4426950408889634)
        kv[...] = dot(normed, wqkv[:, width:]).astype(BF16)
        y = x + dot(attend(query, kv, width), wout[...])
        filler = jnp.zeros((PAD - HALF, width), F32)
        for half in range(2):
            sent[stream, half] = jnp.concatenate([y[half * HALF : (half + 1) * HALF], filler], 0).astype(BF16)

        @pl.when(sec < last)
        def _():
            for half in range(2):
                step_copy(stream, half).start()

        @pl.when(sec == last)
        def _():
            @pl.when(stream == 0)
            def _():
                for c in range(last):
                    pltpu.make_async_copy(whead.at[c], whead.at[c], head_sem.at[c]).wait()

            both = jnp.concatenate([y, jnp.zeros((2 * (PAD - HALF), width), F32)], 0).astype(BF16)
            for pair in range(sections // 2):
                cols = jnp.concatenate([whead[2 * pair], whead[2 * pair + 1]], 1)
                made = dot(both, cols)
                for side in range(2):
                    piece = made[:, side * LANES : (side + 1) * LANES]
                    for half in range(2):
                        rows = piece[half * HALF : half * HALF + PAD]
                        outs[stream, half, 2 * pair + side] = rows.astype(BF16)
                        c = 2 * pair + side
                        if c < last:
                            out_copy(stream, half, c).start()
                        else:
                            pl.when(jnp.logical_not(stays[half]))(out_copy(stream, half, c).start)
                            pl.when(stays[half])(out_local(stream, half, c).start)

        return carry

    lax.fori_loop(0, streams, step, 0)

    @pl.when(sec < LAYERS - SKIP)
    def _():
        def send_skips(stream, carry):
            for half in range(2):
                skip_copy(stream, half).start()
            return carry

        lax.fori_loop(0, streams, send_skips, 0)

    pl.when(sec < 3)(head_copy.start)

    def collect(stream, carry):
        m, lat = stream // 2, lax.rem(stream, 2)
        for half in range(2):
            out_copy(stream, 1 - half, 0).wait_recv()
            halves[half] = outs_in[stream, half].astype(F32)
        for half in range(2):
            for g in range(12):
                joined[g, half * 6 : half * 6 + 6] = halves[half, g * 6 : g * 6 + 6]
        for level in range(2):
            out_ref[m, level, pl.ds(lat * 6, 6)] = joined[level * 6 : level * 6 + 6].astype(BF16)
        return carry

    lax.fori_loop(0, streams, collect, 0)

    def sent_all(stream, carry):
        @pl.when(sec < last)
        def _():
            for half in range(2):
                step_copy(stream, half).wait_send()

        @pl.when(sec < LAYERS - SKIP)
        def _():
            for half in range(2):
                skip_copy(stream, half).wait_send()

        @pl.when(sec == last)
        def _():
            for half in range(2):
                for c in range(sections):
                    if c < last:
                        out_copy(stream, half, c).wait_send()
                    else:
                        pl.when(jnp.logical_not(stays[half]))(out_copy(stream, half, c).wait_send)

        return carry

    lax.fori_loop(0, streams, sent_all, 0)
    pl.when(sec < last)(head_copy.wait_send)


def per_device(inputs, norm_gain, w_qkv, w_out, w_head):
    micro, levels, lat, lon, width = inputs.shape
    sections = lax.axis_size("section")
    columns = w_head.shape[1]
    streams = 2 * micro
    dma = pltpu.SemaphoreType.DMA
    hbm = pl.BlockSpec(memory_space=pl.ANY)
    vmem = pl.BlockSpec(memory_space=pltpu.VMEM)
    return pl.pallas_call(
        functools.partial(kernel, micro),
        out_shape=jax.ShapeDtypeStruct((micro, levels, lat, lon, columns), BF16),
        in_specs=[hbm] * 5,
        out_specs=vmem,
        scratch_shapes=[
            pltpu.VMEM(inputs.shape, BF16),
            pltpu.VMEM(norm_gain.shape, F32),
            pltpu.VMEM(w_qkv.shape[1:], BF16),
            pltpu.VMEM(w_out.shape[1:], BF16),
            pltpu.VMEM((sections,) + w_head.shape, BF16),
            pltpu.VMEM((WIN, width), F32),
            pltpu.VMEM((WIN, 2 * width), BF16),
            pltpu.VMEM((streams, 2, PAD, width), BF16),
            pltpu.VMEM((streams, 2, PAD, width), BF16),
            pltpu.VMEM((streams, 2, PAD, width), BF16),
            pltpu.VMEM((streams, 2, sections, PAD, columns), BF16),
            pltpu.VMEM((streams, 2, PAD, columns), BF16),
            pltpu.VMEM((2, PAD, columns), F32),
            pltpu.VMEM((12, 12, columns), F32),
            dma((5,)),
            dma((streams, 2)),
            dma((streams, 2)),
            dma((streams, 2)),
            dma((streams, 2)),
            dma((sections,)),
            dma,
            dma((streams, 2)),
            dma((streams, 2, sections)),
        ],
        compiler_params=pltpu.CompilerParams(
            collective_id=0, has_side_effects=True, vmem_limit_bytes=40 * 2**20
        ),
    )(inputs, norm_gain, w_qkv, w_out, w_head)


def solution(mesh):
    placed = (
        P(None, None, None, "lon", None),
        P("section", None),
        P("section", None, None),
        P("section", None, None),
        P(None, "section"),
    )
    return jax.shard_map(
        per_device,
        mesh=mesh,
        in_specs=placed,
        out_specs=P(None, None, None, "lon", "section"),
        check_vma=False,
    )
```

```python
import functools

import jax
import jax.numpy as jnp
from jax import lax
from jax.experimental import pallas as pl
from jax.experimental.pallas import tpu as pltpu
from jax.sharding import PartitionSpec as P

MESH = pl.DeviceIdType.MESH
F32, BF16 = jnp.float32, jnp.bfloat16
HEADS = 8
AHEAD = 3
HALF = 72
WIN = 2 * HALF
EPS = 1e-05
LAYERS = 8
SKIP = 5
LAG = 1
LANES = 128


def dot(a, b):
    return jnp.dot(a, b, preferred_element_type=F32)


def dot_t(a, b):
    return lax.dot_general(a, b, (((1,), (1,)), ((), ())), preferred_element_type=F32)


def normalize(x, gain):
    mean = jnp.mean(x, axis=-1, keepdims=True)
    centred = x - mean
    spread = jnp.mean(centred * centred, axis=-1, keepdims=True)
    return (centred * lax.rsqrt(spread + EPS) * gain).astype(BF16)


def attend(query, kv, width):
    rows = query.shape[0]
    low = lax.broadcasted_iota(jnp.int32, (rows, LANES), 1) < LANES // 2
    mixed = []
    for pair in range(width // LANES):
        cols = slice(pair * LANES, (pair + 1) * LANES)
        q = query[:, cols]
        both = jnp.concatenate([jnp.where(low, q, 0.0), jnp.where(low, 0.0, q)], 0).astype(BF16)
        scores = dot_t(both, kv[:, cols])
        top = jnp.max(scores, axis=-1, keepdims=True)
        weights = jnp.exp2(scores - top).astype(BF16)
        values = kv[:, width + pair * LANES : width + (pair + 1) * LANES]
        summed = dot(weights, jnp.concatenate([values, jnp.ones_like(values)], 1))
        summed = summed[:, :LANES] / summed[:, LANES:]
        mixed.append(jnp.where(low, summed[:rows], summed[rows:]))
    return jnp.concatenate(mixed, 1).astype(BF16)


def split(lon, lons):
    low = lax.rem(lon, 2)
    high = lon // (lons // 2)
    return high, lon - low - high * (lons // 2), low


def other(high, low):
    flip = 1 - low
    return high + flip - 2 * high * flip


def holder(layer, block, lons):
    block = lax.rem(block + lons, lons)
    high, middle, low = split(block, lons)
    first = (0, block)
    second = (1, other(high, low) * (lons // 2) + middle + low)
    later = (2 * (layer // 2) + low, block - low + lax.rem(layer, 2))
    return tuple(jnp.where(layer == 0, f, jnp.where(layer == 1, g, h)) for f, g, h in zip(first, second, later))


def role(sec, lon, lons):
    high, middle, low = split(lon, lons)
    side = lax.rem(sec, 2)
    layer = jnp.where(sec < 2, sec, sec - side + low)
    crossed = other(high, low) * (lons // 2) + middle + low
    block = jnp.where(sec == 0, lon, jnp.where(sec == 1, crossed, lon - low + side))
    return layer, block


def kernel(micro, x_ref, gain_ref, wqkv_ref, wout_ref, whead_ref, out_ref,
           xin, gain, wqkv, wout, whead, xs, kv, arrived, skips, relayed, sent, outs,
           load_sem, arrive_sem, send_sem, skip_sem, skipsend_sem, head_sem, headsend_sem, out_sem, outsend_sem,
           swap_sem, swapsend_sem, relay_sem, relaysend_sem):
    sections, lons = lax.axis_size("section"), lax.axis_size("lon")
    sec, lon = lax.axis_index("section"), lax.axis_index("lon")
    layer, mine = role(sec, lon, lons)
    odd = lax.rem(layer, 2)
    width = wout_ref.shape[-1]
    streams = 2 * micro
    last = LAYERS - 1
    core = lax.rem(lon, 2)
    side = lax.rem(sec, 2)
    swaps = jnp.logical_and(sec >= 2, side != core)
    keeps = jnp.logical_not(swaps)

    def target(half, to):
        return holder(to, mine + half - 1 + odd, lons)

    relays = sec >= sections - 2
    from_sec = sec - (sections - 2)
    from_layer, from_block = role(from_sec, lon, lons)

    partners = [(sec + 1 - 2 * side, lax.rem(lon + h * (lons // 2), lons) + 1 - 2 * core) for h in range(2)]

    load_head = pltpu.make_async_copy(whead_ref, whead.at[sec], load_sem.at[3])
    load_head.start()
    load_x = pltpu.make_async_copy(x_ref, xin, load_sem.at[4])
    pl.when(layer == 0)(load_x.start)
    loads = [
        pltpu.make_async_copy(gain_ref, gain, load_sem.at[0]),
        pltpu.make_async_copy(wqkv_ref.at[0], wqkv, load_sem.at[1]),
        pltpu.make_async_copy(wout_ref.at[0], wout, load_sem.at[2]),
    ]

    @pl.when(keeps)
    def _():
        for load in loads:
            load.start()

    barrier = pltpu.get_barrier_semaphore()

    def greet(where):
        pl.semaphore_signal(barrier, inc=1, device_id=where, device_id_type=MESH)

    def source(behind, half):
        before = layer - behind
        return holder(before, mine - (half - 1 + lax.rem(before + LAYERS, 2)), lons)

    @pl.when(layer > 0)
    def _():
        for half in range(2):
            greet(source(1, half))

    @pl.when(layer >= SKIP)
    def _():
        for half in range(2):
            where = source(SKIP, half)
            greet((jnp.where(layer < last, where[0] + sections - 2, where[0]), where[1]))

    pl.when(relays)(lambda: greet((from_sec, lon)))

    @pl.when(swaps)
    def _():
        for where in partners:
            greet(where)

    for half in range(2):
        where = holder(jnp.int32(last), lon - half, lons)
        here = jnp.logical_and(where[0] == sec, where[1] == lon)
        pl.when(jnp.logical_not(here))(functools.partial(greet, where))

    @pl.when(layer == last)
    def _():
        for c in range(sections):
            pl.when(sec != c)(functools.partial(greet, (c, lon)))

    @pl.when(layer == 0)
    def _():
        load_x.wait()

        def place(stream, carry):
            m, lat = stream // 2, lax.rem(stream, 2)
            for half in range(2):
                for a in range(6):
                    block = xin[m, lat * 6 + a, half * 6 : half * 6 + 6].astype(F32)
                    xs[a * 12 : a * 12 + 12] = block.reshape(12, width)
                arrived[stream, half] = xs[:HALF].astype(BF16)
            return carry

        lax.fori_loop(0, streams, place, 0)

    count = jnp.where(layer < last, 2, 2 * sections - 1)
    count = count + jnp.where(layer < 2, 1, jnp.where(layer < LAYERS - SKIP, 2, 0)) + jnp.where(swaps, 2, 0) + jnp.where(relays, 2, 0)
    count = count + jnp.where(core == 1, jnp.where(sec < sections - 2, 2, 1), 0)

    @pl.when(layer > 0)
    @jax.named_scope('greet')
    def _():
        pl.semaphore_wait(barrier, count)

    def swap_copy(half, piece):
        where = partners[half]
        rows = pl.ds(half * (width // 2), width // 2)
        src, dst = ((wqkv_ref.at[0, rows], wqkv.at[rows]), (wout_ref.at[0, rows], wout.at[rows]), (gain_ref, gain))[piece]
        return pltpu.make_async_remote_copy(
            src_ref=src, dst_ref=dst, send_sem=swapsend_sem.at[piece], recv_sem=swap_sem.at[piece],
            device_id=where, device_id_type=MESH)

    swap_list = ((0, 2), (0, 0), (1, 0), (0, 1), (1, 1))

    @pl.when(swaps)
    def _():
        for half, piece in swap_list:
            swap_copy(half, piece).start()

    def swap_wait(sems):
        for piece, ref in enumerate((wqkv, wout, gain)):
            pltpu.make_async_copy(ref, ref, sems.at[piece]).wait()

    def head_copy(b):
        return pltpu.make_async_remote_copy(
            src_ref=whead.at[sec], dst_ref=whead.at[sec], send_sem=headsend_sem.at[b], recv_sem=head_sem,
            device_id=(sections - 2 + b, lon), device_id_type=MESH)

    def each_head(act):
        @pl.when(core == 1)
        def _():
            for b in range(2):
                pl.when(sec != sections - 2 + b)(lambda: act(head_copy(b)))

    load_head.wait()

    @pl.when(keeps)
    def _():
        for load in loads:
            load.wait()

    def step_copy(stream, half):
        return pltpu.make_async_remote_copy(
            src_ref=sent.at[stream, half], dst_ref=arrived.at[stream, 1 - half],
            send_sem=send_sem, recv_sem=arrive_sem.at[stream, 1 - half],
            device_id=target(half, jnp.minimum(layer + 1, last)), device_id_type=MESH)

    def relay_in(stream, half):
        return pltpu.make_async_remote_copy(
            src_ref=sent.at[stream, half], dst_ref=relayed.at[stream, half],
            send_sem=skipsend_sem, recv_sem=relay_sem.at[stream, half],
            device_id=(lax.rem(sec + sections - 2, sections), lon), device_id_type=MESH)

    def relay_out(stream, half):
        return pltpu.make_async_remote_copy(
            src_ref=relayed.at[stream, half], dst_ref=skips.at[stream, 1 - half],
            send_sem=relaysend_sem, recv_sem=skip_sem.at[stream, 1 - half],
            device_id=holder(from_layer + SKIP, from_block + half - 1 + lax.rem(from_layer, 2), lons), device_id_type=MESH)

    def skip_copy(stream, half):
        return pltpu.make_async_remote_copy(
            src_ref=sent.at[stream, half], dst_ref=skips.at[stream, 1 - half],
            send_sem=skipsend_sem, recv_sem=skip_sem.at[stream, 1 - half],
            device_id=target(half, jnp.minimum(layer + SKIP, last)), device_id_type=MESH)

    @jax.named_scope('relay')
    def relay(stream):
        for half in range(2):
            relay_in(stream, half).wait_recv()
            relay_out(stream, half).start()

    def out_copy(stream, half, c):
        return pltpu.make_async_remote_copy(
            src_ref=outs.at[(stream * 2 + half) * sections + c], dst_ref=out_ref.at[stream, 1 - half],
            send_sem=outsend_sem, recv_sem=out_sem,
            device_id=(c, lax.rem(mine + half, lons)), device_id_type=MESH)

    def out_local(stream, half, c):
        return pltpu.make_async_copy(outs.at[(stream * 2 + half) * sections + c], out_ref.at[stream, 1 - half], out_sem)

    def stays(half, c):
        return jnp.logical_and(sec == c, lax.rem(mine + half, lons) == lon)

    def out_side(stream, to):
        def send(row, carry):
            c = 2 * row + to
            for half in range(2):
                pl.when(jnp.logical_not(stays(half, c)))(lambda: out_copy(stream, half, c).start())
                pl.when(stays(half, c))(lambda: out_local(stream, half, c).start())
            return carry

        lax.fori_loop(0, sections // 2, send, 0, unroll=True)

    pl.when(sec >= 4)(lambda: each_head(lambda c: c.start()))

    def relay_some(first, count):
        def one(stream, carry):
            relay(stream)
            return carry

        lax.fori_loop(first, count, one, 0)

    pl.when(sec == sections - 2)(lambda: relay_some(0, streams))
    pl.when(sec == sections - 1)(lambda: relay_some(0, AHEAD))

    def step(stream, carry):
        pl.when(jnp.logical_and(sec == sections - 1, stream < streams - AHEAD))(lambda: relay(stream + AHEAD))

        @pl.when(layer > 0)
        @jax.named_scope('arrive')
        def _():
            for half in range(2):
                step_copy(stream, 1 - half).wait_recv()

        @pl.when(layer < SKIP)
        def _():
            for half in range(2):
                xs[half * HALF : (half + 1) * HALF] = arrived[stream, half].astype(F32)

        @pl.when(layer >= SKIP)
        def _():
            for half in range(2):
                with jax.named_scope('skip'):
                    skip_copy(stream, 1 - half).wait_recv()
                joined = arrived[stream, half].astype(F32) + skips[stream, half].astype(F32)
                xs[half * HALF : (half + 1) * HALF] = joined.astype(BF16).astype(F32)

        first_swapped = jnp.logical_and(swaps, stream == 0)

        @pl.when(first_swapped)
        @jax.named_scope('swap')
        def _():
            swap_wait(swap_sem)

        scope = jax.named_scope('block')
        scope.__enter__()
        x = xs[...]
        normed = normalize(x, gain[...])
        query = dot(normed, wqkv[:, :width]) * ((width // HEADS) ** -0.5 * 1.4426950408889634)
        kv[...] = dot(normed, wqkv[:, width:]).astype(BF16)
        y = x + dot(attend(query, kv, width), wout[...])
        for half in range(2):
            sent[stream, half] = y[half * HALF : (half + 1) * HALF].astype(BF16)

        scope.__exit__(None, None, None)

        @pl.when(jnp.logical_and(layer == 0, stream == 0))
        @jax.named_scope('greet')
        def _():
            pl.semaphore_wait(barrier, count)

        @pl.when(layer < last)
        def _():
            for half in range(2):
                step_copy(stream, half).start()

        @pl.when(layer < 2)
        def _():
            for half in range(2):
                relay_in(stream, half).start()

        @pl.when(layer == 2)
        def _():
            for half in range(2):
                skip_copy(stream, half).start()

        @pl.when(layer == last)
        @jax.named_scope('head')
        def _():
            @pl.when(stream == 0)
            @jax.named_scope('headwait')
            def _():
                others = whead.at[pl.ds(0, sections - 1)]
                pltpu.make_async_copy(others, others, head_sem).wait()

            both = y.astype(BF16)
            for pair in range(sections // 2):
                cols = jnp.concatenate([whead[2 * pair], whead[2 * pair + 1]], 1)
                made = dot(both, cols)
                for part in range(2):
                    piece = made[:, part * LANES : (part + 1) * LANES]
                    for half in range(2):
                        rows = piece[half * HALF : (half + 1) * HALF]
                        outs[(stream * 2 + half) * sections + 2 * pair + part] = rows.astype(BF16)
            out_side(stream, side)
            pl.when(stream >= LAG)(lambda: out_side(stream - LAG, 1 - side))

        return carry

    lax.fori_loop(0, streams, step, 0)

    @pl.when(layer == last)
    def _():
        for late in range(LAG):
            out_side(streams - LAG + late, 1 - side)

    pl.when(sec < 4)(lambda: each_head(lambda c: c.start()))

    with jax.named_scope('output'):
        pltpu.make_async_copy(out_ref, out_ref, out_sem).wait()

    @pl.when(layer < last)
    def _():
        pltpu.make_async_copy(sent, sent, send_sem).wait()

    @pl.when(layer < LAYERS - SKIP)
    def _():
        pltpu.make_async_copy(sent, sent, skipsend_sem).wait()

    @pl.when(relays)
    def _():
        pltpu.make_async_copy(relayed, relayed, relaysend_sem).wait()

    @pl.when(layer == last)
    def _():
        most = outs.at[pl.ds(0, streams * (2 * sections - 1))]
        pltpu.make_async_copy(most, most, outsend_sem).wait()

    each_head(lambda c: c.wait_send())

    @pl.when(swaps)
    def _():
        swap_wait(swapsend_sem)


def per_device(inputs, norm_gain, w_qkv, w_out, w_head):
    inputs = inputs.transpose(0, 2, 3, 1, 4)
    micro, lat, lon, levels, width = inputs.shape
    sections = lax.axis_size("section")
    columns = w_head.shape[1]
    streams = 2 * micro
    dma = pltpu.SemaphoreType.DMA
    hbm = pl.BlockSpec(memory_space=pl.ANY)
    decoded = pl.pallas_call(
        functools.partial(kernel, micro),
        out_shape=jax.ShapeDtypeStruct((streams, 2, HALF, columns), BF16),
        in_specs=[hbm] * 5,
        out_specs=hbm,
        scratch_shapes=[
            pltpu.VMEM(inputs.shape, BF16),
            pltpu.VMEM(norm_gain.shape, F32),
            pltpu.VMEM(w_qkv.shape[1:], BF16),
            pltpu.VMEM(w_out.shape[1:], BF16),
            pltpu.VMEM((sections,) + w_head.shape, BF16),
            pltpu.VMEM((WIN, width), F32),
            pltpu.VMEM((WIN, 2 * width), BF16),
            pltpu.VMEM((streams, 2, HALF, width), BF16),
            pltpu.VMEM((streams, 2, HALF, width), BF16),
            pltpu.VMEM((streams, 2, HALF, width), BF16),
            pltpu.VMEM((streams, 2, HALF, width), BF16),
            pltpu.VMEM((streams * 2 * sections, HALF, columns), BF16),
            dma((5,)),
            dma((streams, 2)),
            dma,
            dma((streams, 2)),
            dma,
            dma,
            dma((2,)),
            dma,
            dma,
            dma((3,)),
            dma((3,)),
            dma((streams, 2)),
            dma,
        ],
        compiler_params=pltpu.CompilerParams(
            collective_id=0, has_side_effects=True, vmem_limit_bytes=60 * 2**20
        ),
    )(inputs, norm_gain, w_qkv, w_out, w_head)
    decoded = decoded.reshape(micro, 2, 2, lat // 2, lon // 2, levels, columns)
    return decoded.transpose(0, 5, 1, 3, 2, 4, 6).reshape(micro, levels, lat, lon, columns)


def solution(mesh):
    placed = (
        P(None, None, None, "lon", None),
        P("section", None),
        P("section", None, None),
        P("section", None, None),
        P(None, "section"),
    )
    return jax.shard_map(
        per_device,
        mesh=mesh,
        in_specs=placed,
        out_specs=P(None, None, None, "lon", "section"),
        check_vma=False,
    )
```

```python
import functools

import jax
import jax.numpy as jnp
from jax import lax
from jax.experimental import pallas as pl
from jax.experimental.pallas import tpu as pltpu
from jax.sharding import PartitionSpec as P

MESH = pl.DeviceIdType.MESH
F32, BF16 = jnp.float32, jnp.bfloat16
HEADS = 8
HALF = 72
WIN = 2 * HALF
EPS = 1e-05
LAYERS = 8
SKIP = 5
LANES = 128


def dot(a, b):
    return jnp.dot(a, b, preferred_element_type=F32)


def dot_t(a, b):
    return lax.dot_general(a, b, (((1,), (1,)), ((), ())), preferred_element_type=F32)


def normalize(x, gain):
    mean = jnp.mean(x, axis=-1, keepdims=True)
    centred = x - mean
    spread = jnp.mean(centred * centred, axis=-1, keepdims=True)
    return (centred * lax.rsqrt(spread + EPS) * gain).astype(BF16)


def attend(query, kv, width):
    rows = query.shape[0]
    low = lax.broadcasted_iota(jnp.int32, (rows, LANES), 1) < LANES // 2
    weights = []
    for pair in range(width // LANES):
        cols = slice(pair * LANES, (pair + 1) * LANES)
        q = query[:, cols]
        both = jnp.concatenate([jnp.where(low, q, 0.0), jnp.where(low, 0.0, q)], 0).astype(BF16)
        scores = dot_t(both, kv[:, cols])
        top = jnp.max(scores, axis=-1, keepdims=True)
        weights.append(jnp.exp2(scores - top).astype(BF16))
    mixed = []
    for pair in range(width // LANES):
        values = kv[:, width + pair * LANES : width + (pair + 1) * LANES]
        summed = dot(weights[pair], jnp.concatenate([values, jnp.ones_like(values)], 1))
        summed = summed[:, :LANES] / summed[:, LANES:]
        mixed.append(jnp.where(low, summed[:rows], summed[rows:]))
    return jnp.concatenate(mixed, 1).astype(BF16)


def split(lon, lons):
    low = lax.rem(lon, 2)
    high = lon // (lons // 2)
    return high, lon - low - high * (lons // 2), low


def crossed(high, middle, low, lons):
    flip = jnp.where(middle == lons // 2 - 2, low, 1 - low)
    return high + flip - 2 * high * flip


def holder(layer, block, lons):
    block = lax.rem(block + lons, lons)
    high, middle, low = split(block, lons)
    first = (0, block)
    second = (1, crossed(high, middle, low, lons) * (lons // 2) + middle + low)
    later = (2 * (layer // 2) + low, block - low + lax.rem(layer, 2))
    return tuple(jnp.where(layer == 0, f, jnp.where(layer == 1, g, h)) for f, g, h in zip(first, second, later))


def role(sec, lon, lons):
    high, middle, low = split(lon, lons)
    side = lax.rem(sec, 2)
    layer = jnp.where(sec < 2, sec, sec - side + low)
    beside = crossed(high, middle, low, lons) * (lons // 2) + middle + low
    block = jnp.where(sec == 0, lon, jnp.where(sec == 1, beside, lon - low + side))
    return layer, block


def kernel(micro, x_ref, gain_ref, wqkv_ref, wout_ref, whead_ref, out_ref,
           xin, gain, wqkv, wout, whead, xs, kv, arrived, skips, relayed, sent, outs,
           load_sem, arrive_sem, send_sem, skip_sem, skipsend_sem, head_sem, headsend_sem, out_sem, outsend_sem,
           swap_sem, swapsend_sem, relay_sem, relaysend_sem, share_sem, sharesend_sem):
    sections, lons = lax.axis_size("section"), lax.axis_size("lon")
    sec, lon = lax.axis_index("section"), lax.axis_index("lon")
    layer, mine = role(sec, lon, lons)
    odd = lax.rem(layer, 2)
    width = wout_ref.shape[-1]
    streams = 2 * micro
    last = LAYERS - 1
    core = lax.rem(lon, 2)
    side = lax.rem(sec, 2)
    swaps = jnp.logical_and(sec >= 2, side != core)
    keeps = jnp.logical_not(swaps)

    def target(half, to):
        return holder(to, mine + half - 1 + odd, lons)

    low = lax.rem(mine, 2)
    from_layer, from_block = role(sec - (sections - 2), lon, lons)
    from_odd = lax.rem(from_block, 2)
    relays = jnp.logical_or(sec == sections - 2, jnp.logical_and(sec == sections - 1, from_odd == 1))
    offers = jnp.logical_or(layer == 0, jnp.logical_and(layer == 1, low == 1))
    straight = sec // 2 == 1

    partners = [(sec + 1 - 2 * side, lax.rem(lon + h * (lons // 2), lons) + 1 - 2 * core) for h in range(2)]

    loads = [
        pltpu.make_async_copy(gain_ref, gain, load_sem.at[0]),
        pltpu.make_async_copy(wqkv_ref.at[0], wqkv, load_sem.at[1]),
        pltpu.make_async_copy(wout_ref.at[0], wout, load_sem.at[2]),
    ]

    def load_x(m):
        return pltpu.make_async_copy(x_ref.at[m], xin.at[m], load_sem.at[4 + m])

    pl.when(layer == 0)(lambda: load_x(0).start())

    @pl.when(keeps)
    def _():
        for load in loads:
            load.start()

    load_head = pltpu.make_async_copy(whead_ref, whead.at[side, sec // 2], load_sem.at[3])

    barrier = pltpu.get_barrier_semaphore()

    def greet(where):
        pl.semaphore_signal(barrier, inc=1, device_id=where, device_id_type=MESH)

    def source(behind, half):
        before = layer - behind
        return holder(before, mine - (half - 1 + lax.rem(before + LAYERS, 2)), lons)

    @pl.when(layer > 0)
    def _():
        for half in range(2):
            greet(source(1, half))

    @pl.when(jnp.logical_and(layer == SKIP, low == 0))
    def _():
        greet((sections - 2, mine))
        greet((sections - 2, mine + 1))

    pl.when(jnp.logical_and(layer == SKIP, low == 1))(lambda: greet((sections - 1, holder(jnp.int32(1), mine, lons)[1])))
    pl.when(layer > SKIP)(lambda: greet((sec - 4, lon)))
    pl.when(relays)(lambda: greet((sec - (sections - 2), lon)))

    @pl.when(swaps)
    def _():
        for where in partners:
            greet(where)

    for half in range(2):
        where = holder(jnp.int32(last), lon - half, lons)
        here = jnp.logical_and(where[0] == sec, where[1] == lon)
        pl.when(jnp.logical_not(here))(functools.partial(greet, where))

    @pl.when(layer == last)
    def _():
        for row in range(sections // 2 - 1):
            greet((2 * row + side, lon))
        greet((sec + 1 - 2 * side, lon))

    def place(stream):
        m, lat = stream // 2, lax.rem(stream, 2)
        pl.when(lat == 0)(lambda: load_x(m).wait())
        for half in range(2):
            for a in range(6):
                block = xin[m, lat * 6 + a, half * 6 : half * 6 + 6].astype(F32)
                at = half * HALF + a * 12
                xs[at : at + 12] = block.reshape(12, width)

    count = jnp.where(layer < last, 2, 2 * sections - 1) + jnp.where(swaps, 2, 0)
    for sends in (offers, straight, relays, core == 1):
        count = count + jnp.where(sends, 1, 0)

    @pl.when(layer > 0)
    @jax.named_scope('greet')
    def _():
        pl.semaphore_wait(barrier, count)

    def swap_copy(half, piece):
        where = partners[half]
        rows = pl.ds(half * (width // 2), width // 2)
        src, dst = ((wqkv_ref.at[0, rows], wqkv.at[rows]), (wout_ref.at[0, rows], wout.at[rows]), (gain_ref, gain))[piece]
        return pltpu.make_async_remote_copy(
            src_ref=src, dst_ref=dst, send_sem=swapsend_sem.at[piece], recv_sem=swap_sem.at[piece],
            device_id=where, device_id_type=MESH)

    swap_list = ((0, 2), (0, 0), (1, 0), (0, 1), (1, 1))

    @pl.when(swaps)
    def _():
        for half, piece in swap_list:
            swap_copy(half, piece).start()

    def swap_wait(sems, piece):
        ref = (wqkv, wout, gain)[piece]
        pltpu.make_async_copy(ref, ref, sems.at[piece]).wait()

    def head_copy():
        mine_head = whead.at[side, sec // 2]
        return pltpu.make_async_remote_copy(
            src_ref=mine_head, dst_ref=mine_head, send_sem=headsend_sem, recv_sem=head_sem,
            device_id=(sections - 2 + side, lon), device_id_type=MESH)

    def share_copy():
        return pltpu.make_async_remote_copy(
            src_ref=whead.at[side], dst_ref=whead.at[side], send_sem=sharesend_sem, recv_sem=share_sem,
            device_id=(sec + 1 - 2 * side, lon), device_id_type=MESH)

    sends_head = jnp.logical_and(core == 1, sec < sections - 2)


    @pl.when(keeps)
    def _():
        for load in loads:
            load.wait()

    load_head.start()

    @pl.when(layer == 0)
    def _():
        for m in range(1, micro):
            load_x(m).start()

    def step_copy(stream, half):
        return pltpu.make_async_remote_copy(
            src_ref=sent.at[stream, half], dst_ref=arrived.at[stream, 1 - half],
            send_sem=send_sem, recv_sem=arrive_sem.at[stream, 1 - half],
            device_id=target(half, jnp.minimum(layer + 1, last)), device_id_type=MESH)

    def offer_one(stream):
        return pltpu.make_async_remote_copy(
            src_ref=sent.at[stream, 1 - low], dst_ref=relayed.at[stream, 0],
            send_sem=skipsend_sem, recv_sem=relay_sem.at[stream, 0],
            device_id=(sections - 2, lon), device_id_type=MESH)

    def offer_both(stream, half):
        return pltpu.make_async_remote_copy(
            src_ref=arrived.at[stream, half], dst_ref=relayed.at[stream, half],
            send_sem=skipsend_sem, recv_sem=relay_sem.at[stream, half],
            device_id=(sections - 1, lon), device_id_type=MESH)

    def relay_out(stream, half, slot, block):
        return pltpu.make_async_remote_copy(
            src_ref=relayed.at[stream, half], dst_ref=skips.at[stream, slot],
            send_sem=relaysend_sem, recv_sem=skip_sem.at[stream, slot],
            device_id=holder(jnp.int32(SKIP), block, lons), device_id_type=MESH)

    def skip_copy(stream, half):
        return pltpu.make_async_remote_copy(
            src_ref=arrived.at[stream, half], dst_ref=skips.at[stream, half],
            send_sem=skipsend_sem, recv_sem=skip_sem.at[stream, half],
            device_id=(lax.rem(sec + 4, sections), lon), device_id_type=MESH)

    @jax.named_scope('relay')
    def relay(stream):
        @pl.when(sec == sections - 2)
        def _():
            offer_one(stream).wait_recv()
            relay_out(stream, 0, from_odd, from_block - from_odd).start()

        @pl.when(sec == sections - 1)
        def _():
            for half in range(2):
                offer_both(stream, half).wait_recv()
                relay_out(stream, half, half, from_block).start()

    def out_copy(stream, half, c):
        return pltpu.make_async_remote_copy(
            src_ref=outs.at[(stream * 2 + half) * sections + c], dst_ref=out_ref.at[stream, 1 - half],
            send_sem=outsend_sem, recv_sem=out_sem,
            device_id=(c, lax.rem(mine + half, lons)), device_id_type=MESH)

    def out_local(stream, half, c):
        return pltpu.make_async_copy(outs.at[(stream * 2 + half) * sections + c], out_ref.at[stream, 1 - half], out_sem)

    def stays(half, c):
        return jnp.logical_and(sec == c, lax.rem(mine + half, lons) == lon)

    def out_side(stream, to):
        def send(row, carry):
            c = 2 * row + to
            for half in range(2):
                pl.when(jnp.logical_not(stays(half, c)))(lambda: out_copy(stream, half, c).start())
                pl.when(stays(half, c))(lambda: out_local(stream, half, c).start())
            return carry

        lax.fori_loop(0, sections // 2, send, 0, unroll=True)

    def send_head():
        load_head.wait()
        pl.when(sends_head)(lambda: head_copy().start())

    pl.when(layer > 0)(send_head)

    @pl.when(layer == last)
    @jax.named_scope('share')
    def _():
        others = whead.at[side, pl.ds(0, sections // 2 - 1)]
        pltpu.make_async_copy(others, others, head_sem).wait()
        share_copy().start()

    def relay_all():
        def one(stream, carry):
            relay(stream)
            return carry

        lax.fori_loop(0, streams, one, 0)

    pl.when(relays)(relay_all)

    def step(stream, carry):
        @pl.when(layer > 0)
        @jax.named_scope('arrive')
        def _():
            for half in range(2):
                step_copy(stream, 1 - half).wait_recv()

        pl.when(layer == 0)(lambda: place(stream))

        @pl.when(jnp.logical_and(layer == 1, low == 1))
        def _():
            for half in range(2):
                offer_both(stream, half).start()

        @pl.when(straight)
        def _():
            for half in range(2):
                skip_copy(stream, half).start()

        @pl.when(jnp.logical_and(layer > 0, layer < SKIP))
        def _():
            for half in range(2):
                xs[half * HALF : (half + 1) * HALF] = arrived[stream, half].astype(F32)

        @pl.when(layer >= SKIP)
        def _():
            for half in range(2):
                with jax.named_scope('skip'):
                    skip_copy(stream, half).wait_recv()
                joined = arrived[stream, half].astype(F32) + skips[stream, half].astype(F32)
                xs[half * HALF : (half + 1) * HALF] = joined.astype(BF16).astype(F32)

        def block(before_out):
            x = xs[...]
            normed = normalize(x, gain[...])
            query = dot(normed, wqkv[:, :width]) * ((width // HEADS) ** -0.5 * 1.4426950408889634)
            kv[...] = dot(normed, wqkv[:, width:]).astype(BF16)
            mixed = attend(query, kv, width)
            before_out()
            y = x + dot(mixed, wout[...])
            for half in range(2):
                sent[stream, half] = y[half * HALF : (half + 1) * HALF].astype(BF16)

        first_swapped = jnp.logical_and(swaps, stream == 0)

        @pl.when(first_swapped)
        def _():
            with jax.named_scope('swap'):
                swap_wait(swap_sem, 0)
                swap_wait(swap_sem, 2)
            block(lambda: swap_wait(swap_sem, 1))

        @pl.when(jnp.logical_not(first_swapped))
        @jax.named_scope('block')
        def _():
            block(lambda: None)

        @pl.when(jnp.logical_and(layer == 0, stream == 0))
        @jax.named_scope('greet')
        def _():
            pl.semaphore_wait(barrier, count)

        @pl.when(layer < last)
        def _():
            for half in range(2):
                step_copy(stream, half).start()

        pl.when(layer == 0)(lambda: offer_one(stream).start())
        pl.when(jnp.logical_and(layer == 0, stream == 0))(send_head)

        @pl.when(layer == last)
        @jax.named_scope('head')
        def _():
            @pl.when(stream == 0)
            @jax.named_scope('headwait')
            def _():
                share_copy().wait_recv()

            both = jnp.concatenate([sent[stream, 0].astype(F32), sent[stream, 1].astype(F32)], 0).astype(BF16)
            for pair in range(sections // 2):
                cols = jnp.concatenate([whead[0, pair], whead[1, pair]], 1)
                made = dot(both, cols)
                for part in range(2):
                    piece = made[:, part * LANES : (part + 1) * LANES]
                    for half in range(2):
                        rows = piece[half * HALF : (half + 1) * HALF]
                        outs[(stream * 2 + half) * sections + 2 * pair + part] = rows.astype(BF16)
            pl.when(jnp.logical_and(stream >= 1, stream < streams - 1))(lambda: out_side(stream - 1, 1 - side))
            pl.when(stream >= streams - 2)(lambda: out_side(stream, 1 - side))
            out_side(stream, side)

        return carry

    lax.fori_loop(0, streams, step, 0)

    with jax.named_scope('output'):
        pltpu.make_async_copy(out_ref, out_ref, out_sem).wait()

    @pl.when(layer < last)
    def _():
        pltpu.make_async_copy(sent, sent, send_sem).wait()

    def left(ref, sem):
        pltpu.make_async_copy(ref, ref, sem).wait()

    one_each = pl.ds(0, streams // 2)
    pl.when(layer == 0)(lambda: left(sent.at[one_each], skipsend_sem))
    pl.when(jnp.logical_or(straight, jnp.logical_and(offers, layer == 1)))(lambda: left(arrived, skipsend_sem))
    pl.when(sec == sections - 2)(lambda: left(relayed.at[one_each], relaysend_sem))
    pl.when(jnp.logical_and(relays, sec == sections - 1))(lambda: left(relayed, relaysend_sem))

    @pl.when(layer == last)
    def _():
        most = outs.at[pl.ds(0, streams * (2 * sections - 1))]
        pltpu.make_async_copy(most, most, outsend_sem).wait()

    pl.when(sends_head)(lambda: head_copy().wait_send())

    @pl.when(layer == last)
    def _():
        share_copy().wait_send()

    @pl.when(swaps)
    def _():
        for piece in range(3):
            swap_wait(swapsend_sem, piece)


def per_device(inputs, norm_gain, w_qkv, w_out, w_head):
    inputs = inputs.transpose(0, 2, 3, 1, 4)
    micro, lat, lon, levels, width = inputs.shape
    sections = lax.axis_size("section")
    columns = w_head.shape[1]
    streams = 2 * micro
    dma = pltpu.SemaphoreType.DMA
    hbm = pl.BlockSpec(memory_space=pl.ANY)
    decoded = pl.pallas_call(
        functools.partial(kernel, micro),
        out_shape=jax.ShapeDtypeStruct((streams, 2, HALF, columns), BF16),
        in_specs=[hbm] * 5,
        out_specs=hbm,
        scratch_shapes=[
            pltpu.VMEM(inputs.shape, BF16),
            pltpu.VMEM(norm_gain.shape, F32),
            pltpu.VMEM(w_qkv.shape[1:], BF16),
            pltpu.VMEM(w_out.shape[1:], BF16),
            pltpu.VMEM((2, sections // 2) + w_head.shape, BF16),
            pltpu.VMEM((WIN, width), F32),
            pltpu.VMEM((WIN, 2 * width), BF16),
            pltpu.VMEM((streams, 2, HALF, width), BF16),
            pltpu.VMEM((streams, 2, HALF, width), BF16),
            pltpu.VMEM((streams, 2, HALF, width), BF16),
            pltpu.VMEM((streams, 2, HALF, width), BF16),
            pltpu.VMEM((streams * 2 * sections, HALF, columns), BF16),
            dma((4 + micro,)),
            dma((streams, 2)),
            dma,
            dma((streams, 2)),
            dma,
            dma,
            dma,
            dma,
            dma,
            dma((3,)),
            dma((3,)),
            dma((streams, 2)),
            dma,
            dma,
            dma,
        ],
        compiler_params=pltpu.CompilerParams(
            collective_id=0, has_side_effects=True, vmem_limit_bytes=60 * 2**20
        ),
    )(inputs, norm_gain, w_qkv, w_out, w_head)
    decoded = decoded.reshape(micro, 2, 2, lat // 2, lon // 2, levels, columns)
    return decoded.transpose(0, 5, 1, 3, 2, 4, 6).reshape(micro, levels, lat, lon, columns)


def solution(mesh):
    placed = (
        P(None, None, None, "lon", None),
        P("section", None),
        P("section", None, None),
        P("section", None, None),
        P(None, "section"),
    )
    return jax.shard_map(
        per_device,
        mesh=mesh,
        in_specs=placed,
        out_specs=P(None, None, None, "lon", "section"),
        check_vma=False,
    )
```

```python
import functools

import jax
import jax.numpy as jnp
from jax import lax
from jax.experimental import pallas as pl
from jax.experimental.pallas import tpu as pltpu
from jax.sharding import PartitionSpec as P

MESH = pl.DeviceIdType.MESH
F32, BF16 = jnp.float32, jnp.bfloat16
HEADS = 8
PASSED = 4
HALF = 72
WIN = 2 * HALF
EPS = 1e-05
LAYERS = 8
SKIP = 5
LANES = 128


def dot(a, b):
    return jnp.dot(a, b, preferred_element_type=F32)


def dot_t(a, b):
    return lax.dot_general(a, b, (((1,), (1,)), ((), ())), preferred_element_type=F32)


def normalize(x, gain):
    mean = jnp.mean(x, axis=-1, keepdims=True)
    centred = x - mean
    spread = jnp.mean(centred * centred, axis=-1, keepdims=True)
    return (centred * lax.rsqrt(spread + EPS) * gain).astype(BF16)


def attend(query, kv, width):
    rows = query.shape[0]
    low = lax.broadcasted_iota(jnp.int32, (rows, LANES), 1) < LANES // 2
    weights = []
    for pair in range(width // LANES):
        cols = slice(pair * LANES, (pair + 1) * LANES)
        q = query[:, cols]
        both = jnp.concatenate([jnp.where(low, q, 0.0), jnp.where(low, 0.0, q)], 0).astype(BF16)
        scores = dot_t(both, kv[:, cols])
        top = jnp.max(scores, axis=-1, keepdims=True)
        weights.append(jnp.exp2(scores - top).astype(BF16))
    mixed = []
    for pair in range(width // LANES):
        values = kv[:, width + pair * LANES : width + (pair + 1) * LANES]
        summed = dot(weights[pair], jnp.concatenate([values, jnp.ones_like(values)], 1))
        summed = summed[:, :LANES] / summed[:, LANES:]
        mixed.append(jnp.where(low, summed[:rows], summed[rows:]))
    return jnp.concatenate(mixed, 1).astype(BF16)


def split(lon, lons):
    low = lax.rem(lon, 2)
    high = lon // (lons // 2)
    return high, lon - low - high * (lons // 2), low


def beside(high, middle, low, lons):
    flip = 1 - low
    usual = (high + flip - 2 * high * flip) * (lons // 2) + middle + low
    return usual, middle == lons // 2 - 2


def from_first(block, lons):
    _, middle, low = split(lax.rem(block + lons, lons), lons)
    return jnp.logical_or(low == 0, middle == lons // 2 - 2)


def holder(layer, block, lons):
    block = lax.rem(block + lons, lons)
    high, middle, low = split(block, lons)
    first = (0, block)
    usual, at_end = beside(high, middle, low, lons)
    second = (1, jnp.where(at_end, (1 - low) * (lons // 2) + middle + high, usual))
    later = (2 * (layer // 2) + low, block - low + lax.rem(layer, 2))
    return tuple(jnp.where(layer == 0, f, jnp.where(layer == 1, g, h)) for f, g, h in zip(first, second, later))


def role(sec, lon, lons):
    high, middle, low = split(lon, lons)
    side = lax.rem(sec, 2)
    layer = jnp.where(sec < 2, sec, sec - side + low)
    usual, at_end = beside(high, middle, low, lons)
    second = jnp.where(at_end, low * (lons // 2) + middle + 1 - high, usual)
    block = jnp.where(sec == 0, lon, jnp.where(sec == 1, second, lon - low + side))
    return layer, block


def kernel(micro, x_ref, gain_ref, wqkv_ref, wout_ref, whead_ref, out_ref,
           xin, gain, wqkv, wout, whead, xs, kv, arrived, skips, relayed, sent, outs, passed,
           load_sem, arrive_sem, send_sem, skip_sem, skipsend_sem, head_sem, headsend_sem, out_sem, outsend_sem,
           swap_sem, swapsend_sem, relay_sem, relaysend_sem, share_sem, sharesend_sem, pass_sem, passsend_sem):
    sections, lons = lax.axis_size("section"), lax.axis_size("lon")
    sec, lon = lax.axis_index("section"), lax.axis_index("lon")
    layer, mine = role(sec, lon, lons)
    odd = lax.rem(layer, 2)
    width = wout_ref.shape[-1]
    streams = 2 * micro
    last = LAYERS - 1
    core = lax.rem(lon, 2)
    side = lax.rem(sec, 2)
    swaps = jnp.logical_and(sec >= 2, side != core)
    keeps = jnp.logical_not(swaps)

    def target(half, to):
        return holder(to, mine + half - 1 + odd, lons)

    from_layer, from_block = role(sec - (sections - 2), lon, lons)

    def given(block):
        return [from_first(block + half - 1, lons) for half in range(2)]

    gives = [jnp.logical_and(layer == 0, g) for g in given(mine)]
    hands = [jnp.logical_and(sec == sections - 2, g) for g in given(from_block)]
    gives_input = jnp.logical_and(layer == 1, jnp.logical_not(from_first(mine, lons)))
    hands_input = jnp.logical_and(sec == sections - 1, jnp.logical_not(from_first(from_block, lons)))
    offers = jnp.logical_or(layer == 0, gives_input)
    relays = jnp.logical_or(sec == sections - 2, hands_input)
    straight = sec // 2 == 1

    partners = [(sec + 1 - 2 * side, lax.rem(lon + h * (lons // 2), lons) + 1 - 2 * core) for h in range(2)]

    loads = [
        pltpu.make_async_copy(gain_ref, gain, load_sem.at[0]),
        pltpu.make_async_copy(wqkv_ref.at[0], wqkv, load_sem.at[1]),
        pltpu.make_async_copy(wout_ref.at[0], wout, load_sem.at[2]),
    ]

    def load_x(m):
        return pltpu.make_async_copy(x_ref.at[m], xin.at[m], load_sem.at[4 + m])

    pl.when(layer == 0)(lambda: load_x(0).start())

    @pl.when(keeps)
    def _():
        loads[0].start()
        rows = width // 4
        for part in range(4):
            at = pl.ds(part * rows, rows)
            pltpu.make_async_copy(wqkv_ref.at[0, at], wqkv.at[at], load_sem.at[1]).start()
        loads[2].start()

    load_head = pltpu.make_async_copy(whead_ref, whead.at[side, sec // 2], load_sem.at[3])

    barrier = pltpu.get_barrier_semaphore()

    def greet(where):
        pl.semaphore_signal(barrier, inc=1, device_id=where, device_id_type=MESH)

    def source(behind, half):
        before = layer - behind
        return holder(before, mine - (half - 1 + lax.rem(before + LAYERS, 2)), lons)

    @pl.when(layer > 0)
    def _():
        for half in range(2):
            greet(source(1, half))

    @pl.when(jnp.logical_and(layer == SKIP, from_first(mine, lons)))
    def _():
        greet((sections - 2, mine))
        greet((sections - 2, lax.rem(mine + 1, lons)))

    @pl.when(jnp.logical_and(layer == SKIP, jnp.logical_not(from_first(mine, lons))))
    def _():
        greet((sections - 1, holder(jnp.int32(1), mine, lons)[1]))

    pl.when(layer > SKIP)(lambda: greet((sec - 4, lon)))
    pl.when(relays)(lambda: greet((sec - (sections - 2), lon)))
    passes = sec < sections - 2
    pl.when(passes)(lambda: greet((sec + 1 - 2 * side, lon)))

    @pl.when(swaps)
    def _():
        for where in partners:
            greet(where)

    for half in range(2):
        where = holder(jnp.int32(last), lon - half, lons)
        here = jnp.logical_and(where[0] == sec, where[1] == lon)
        pl.when(jnp.logical_not(here))(functools.partial(greet, where))

    @pl.when(layer == last)
    def _():
        for row in range(sections // 2 - 1):
            greet((2 * row + side, lon))
        greet((sec + 1 - 2 * side, lon))

    def place(stream):
        m, lat = stream // 2, lax.rem(stream, 2)
        pl.when(lat == 0)(lambda: load_x(m).wait())
        for half in range(2):
            for a in range(6):
                block = xin[m, lat * 6 + a, half * 6 : half * 6 + 6].astype(F32)
                at = half * HALF + a * 12
                xs[at : at + 12] = block.reshape(12, width)

    count = jnp.where(layer < last, 2, 2 * sections - 1) + jnp.where(swaps, 2, 0)
    for sends in (offers, straight, hands[0], hands[1], hands_input, passes, core == 1):
        count = count + jnp.where(sends, 1, 0)

    @pl.when(layer > 0)
    @jax.named_scope('greet')
    def _():
        pl.semaphore_wait(barrier, count)

    def swap_copy(half, piece):
        where = partners[half]
        rows = pl.ds(half * (width // 2), width // 2)
        src, dst = ((wqkv_ref.at[0, rows], wqkv.at[rows]), (wout_ref.at[0, rows], wout.at[rows]), (gain_ref, gain))[piece]
        return pltpu.make_async_remote_copy(
            src_ref=src, dst_ref=dst, send_sem=swapsend_sem.at[piece], recv_sem=swap_sem.at[piece],
            device_id=where, device_id_type=MESH)

    swap_list = ((0, 2), (0, 0), (1, 0), (0, 1), (1, 1))

    @pl.when(swaps)
    def _():
        for half, piece in swap_list:
            swap_copy(half, piece).start()

    def swap_wait(sems, piece):
        ref = (wqkv, wout, gain)[piece]
        pltpu.make_async_copy(ref, ref, sems.at[piece]).wait()

    def head_copy():
        mine_head = whead.at[side, sec // 2]
        return pltpu.make_async_remote_copy(
            src_ref=mine_head, dst_ref=mine_head, send_sem=headsend_sem, recv_sem=head_sem,
            device_id=(sections - 2 + side, lon), device_id_type=MESH)

    def share_copy():
        return pltpu.make_async_remote_copy(
            src_ref=whead.at[side], dst_ref=whead.at[side], send_sem=sharesend_sem, recv_sem=share_sem,
            device_id=(sec + 1 - 2 * side, lon), device_id_type=MESH)

    sends_head = jnp.logical_and(core == 1, sec < sections - 2)


    @pl.when(keeps)
    def _():
        for load in loads:
            load.wait()

    load_head.start()

    @pl.when(layer == 0)
    def _():
        for m in range(1, micro):
            load_x(m).start()

    def step_copy(stream, half):
        return pltpu.make_async_remote_copy(
            src_ref=sent.at[stream, half], dst_ref=arrived.at[stream, 1 - half],
            send_sem=send_sem, recv_sem=arrive_sem.at[stream, 1 - half],
            device_id=target(half, jnp.minimum(layer + 1, last)), device_id_type=MESH)

    def offer(ref, stream, half):
        return pltpu.make_async_remote_copy(
            src_ref=ref.at[stream, half], dst_ref=relayed.at[stream, half],
            send_sem=skipsend_sem, recv_sem=relay_sem.at[stream, half],
            device_id=(lax.rem(sec + sections - 2, sections), lon), device_id_type=MESH)

    def relay_out(stream, half, slot, block):
        return pltpu.make_async_remote_copy(
            src_ref=relayed.at[stream, half], dst_ref=skips.at[stream, slot],
            send_sem=relaysend_sem, recv_sem=skip_sem.at[stream, slot],
            device_id=holder(jnp.int32(SKIP), block, lons), device_id_type=MESH)

    def skip_copy(stream, half):
        return pltpu.make_async_remote_copy(
            src_ref=arrived.at[stream, half], dst_ref=skips.at[stream, half],
            send_sem=skipsend_sem, recv_sem=skip_sem.at[stream, half],
            device_id=(lax.rem(sec + 4, sections), lon), device_id_type=MESH)

    @jax.named_scope('relay')
    def relay(stream):
        for half in range(2):
            @pl.when(hands[half])
            def _():
                offer(sent, stream, half).wait_recv()
                relay_out(stream, half, 1 - half, from_block + half - 1).start()

        @pl.when(hands_input)
        def _():
            for half in range(2):
                offer(arrived, stream, half).wait_recv()
                relay_out(stream, half, half, from_block).start()

    def out_copy(stream, half, c):
        return pltpu.make_async_remote_copy(
            src_ref=outs.at[(stream * 2 + half) * sections + c], dst_ref=out_ref.at[stream, 1 - half],
            send_sem=outsend_sem, recv_sem=out_sem,
            device_id=(c, lax.rem(mine + half, lons)), device_id_type=MESH)

    def out_local(stream, half, c):
        return pltpu.make_async_copy(outs.at[(stream * 2 + half) * sections + c], out_ref.at[stream, 1 - half], out_sem)

    def stays(half, c):
        return jnp.logical_and(sec == c, lax.rem(mine + half, lons) == lon)

    def out_side(stream, to, rows=range(sections // 2)):
        for row in rows:
            c = 2 * row + to
            for half in range(2):
                pl.when(jnp.logical_not(stays(half, c)))(lambda: out_copy(stream, half, c).start())
                pl.when(stays(half, c))(lambda: out_local(stream, half, c).start())

    def pass_in(stream, half, row):
        c = 2 * row + 1 - side
        return pltpu.make_async_remote_copy(
            src_ref=outs.at[(stream * 2 + half) * sections + c], dst_ref=passed.at[stream],
            send_sem=outsend_sem, recv_sem=pass_sem.at[stream],
            device_id=(2 * row + side, lax.rem(mine + half, lons)), device_id_type=MESH)

    def pass_out(stream):
        slot = jnp.where(core == side, 1, 0)
        return pltpu.make_async_remote_copy(
            src_ref=passed.at[stream], dst_ref=out_ref.at[stream, slot], send_sem=passsend_sem, recv_sem=out_sem,
            device_id=(sec + 1 - 2 * side, lon), device_id_type=MESH)

    def send_head():
        load_head.wait()
        pl.when(sends_head)(lambda: head_copy().start())

    pl.when(layer > 0)(send_head)

    @pl.when(layer == last)
    @jax.named_scope('share')
    def _():
        others = whead.at[side, pl.ds(0, sections // 2 - 1)]
        pltpu.make_async_copy(others, others, head_sem).wait()
        share_copy().start()

    def relay_all():
        def one(stream, carry):
            relay(stream)
            return carry

        lax.fori_loop(0, streams, one, 0)

    pl.when(relays)(relay_all)

    def step(stream, carry):
        @pl.when(layer > 0)
        @jax.named_scope('arrive')
        def _():
            for half in range(2):
                step_copy(stream, 1 - half).wait_recv()

        pl.when(layer == 0)(lambda: place(stream))

        @pl.when(gives_input)
        def _():
            for half in range(2):
                offer(arrived, stream, half).start()


        @pl.when(jnp.logical_and(layer > 0, layer < SKIP))
        def _():
            for half in range(2):
                xs[half * HALF : (half + 1) * HALF] = arrived[stream, half].astype(F32)

        @pl.when(layer >= SKIP)
        def _():
            for half in range(2):
                with jax.named_scope('skip'):
                    skip_copy(stream, half).wait_recv()
                joined = arrived[stream, half].astype(F32) + skips[stream, half].astype(F32)
                xs[half * HALF : (half + 1) * HALF] = joined.astype(BF16).astype(F32)

        def block(before_out):
            x = xs[...]
            normed = normalize(x, gain[...])
            query = dot(normed, wqkv[:, :width]) * ((width // HEADS) ** -0.5 * 1.4426950408889634)
            kv[...] = dot(normed, wqkv[:, width:]).astype(BF16)
            mixed = attend(query, kv, width)
            before_out()
            y = x + dot(mixed, wout[...])
            for half in range(2):
                sent[stream, half] = y[half * HALF : (half + 1) * HALF].astype(BF16)

        first_swapped = jnp.logical_and(swaps, stream == 0)

        @pl.when(first_swapped)
        def _():
            with jax.named_scope('swap'):
                swap_wait(swap_sem, 0)
                swap_wait(swap_sem, 2)
            block(lambda: swap_wait(swap_sem, 1))

        @pl.when(jnp.logical_not(first_swapped))
        @jax.named_scope('block')
        def _():
            block(lambda: None)

        @pl.when(jnp.logical_and(layer == 0, stream == 0))
        @jax.named_scope('greet')
        def _():
            pl.semaphore_wait(barrier, count)

        @pl.when(layer < last)
        def _():
            for half in range(2):
                step_copy(stream, half).start()

        for half in range(2):
            pl.when(gives[half])(offer(sent, stream, half).start)

        pl.when(jnp.logical_and(layer == 0, stream == 0))(send_head)

        @pl.when(layer == last)
        @jax.named_scope('head')
        def _():
            @pl.when(stream == 0)
            @jax.named_scope('headwait')
            def _():
                share_copy().wait_recv()

            both = jnp.concatenate([sent[stream, 0].astype(F32), sent[stream, 1].astype(F32)], 0).astype(BF16)
            for pair in range(sections // 2):
                cols = jnp.concatenate([whead[0, pair], whead[1, pair]], 1)
                made = dot(both, cols)
                for part in range(2):
                    piece = made[:, part * LANES : (part + 1) * LANES]
                    for half in range(2):
                        rows = piece[half * HALF : (half + 1) * HALF]
                        outs[(stream * 2 + half) * sections + 2 * pair + part] = rows.astype(BF16)
            @pl.when(stream < PASSED)
            def _():
                for row in range(sections // 2 - 1):
                    for half in range(2):
                        pass_in(stream, half, row).start()
                out_side(stream, 1 - side, [sections // 2 - 1])

            pl.when(stream >= PASSED)(lambda: out_side(stream, 1 - side))
            out_side(stream, side)

        return carry

    lax.fori_loop(0, streams, step, 0)

    @pl.when(straight)
    def _():
        def send_skips(stream, carry):
            for half in range(2):
                skip_copy(stream, half).start()
            return carry

        lax.fori_loop(0, streams, send_skips, 0)

    @pl.when(passes)
    @jax.named_scope('pass')
    def _():
        def hand(stream, carry):
            pltpu.make_async_copy(passed.at[stream], passed.at[stream], pass_sem.at[stream]).wait()
            pass_out(stream).start()
            return carry

        lax.fori_loop(0, PASSED, hand, 0)

    with jax.named_scope('output'):
        pltpu.make_async_copy(out_ref, out_ref, out_sem).wait()

    @pl.when(layer < last)
    def _():
        pltpu.make_async_copy(sent, sent, send_sem).wait()

    def left(ref, sem):
        pltpu.make_async_copy(ref, ref, sem).wait()

    pl.when(passes)(lambda: left(passed, passsend_sem))
    def left_halves(ref, sem, which):
        one, both = jnp.logical_xor(*which), jnp.logical_and(*which)
        pl.when(one)(lambda: left(ref.at[pl.ds(0, streams // 2)], sem))
        pl.when(both)(lambda: left(ref, sem))

    left_halves(sent, skipsend_sem, gives)
    left_halves(relayed, relaysend_sem, hands)
    pl.when(jnp.logical_or(straight, gives_input))(lambda: left(arrived, skipsend_sem))
    pl.when(hands_input)(lambda: left(relayed, relaysend_sem))

    @pl.when(layer == last)
    def _():
        most = outs.at[pl.ds(0, streams * (2 * sections - 1))]
        pltpu.make_async_copy(most, most, outsend_sem).wait()

    pl.when(sends_head)(lambda: head_copy().wait_send())

    @pl.when(layer == last)
    def _():
        share_copy().wait_send()

    @pl.when(swaps)
    def _():
        for piece in range(3):
            swap_wait(swapsend_sem, piece)


def per_device(inputs, norm_gain, w_qkv, w_out, w_head):
    inputs = inputs.transpose(0, 2, 3, 1, 4)
    micro, lat, lon, levels, width = inputs.shape
    sections = lax.axis_size("section")
    columns = w_head.shape[1]
    streams = 2 * micro
    dma = pltpu.SemaphoreType.DMA
    hbm = pl.BlockSpec(memory_space=pl.ANY)
    decoded = pl.pallas_call(
        functools.partial(kernel, micro),
        out_shape=jax.ShapeDtypeStruct((streams, 2, HALF, columns), BF16),
        in_specs=[hbm] * 5,
        out_specs=hbm,
        scratch_shapes=[
            pltpu.VMEM(inputs.shape, BF16),
            pltpu.VMEM(norm_gain.shape, F32),
            pltpu.VMEM(w_qkv.shape[1:], BF16),
            pltpu.VMEM(w_out.shape[1:], BF16),
            pltpu.VMEM((2, sections // 2) + w_head.shape, BF16),
            pltpu.VMEM((WIN, width), F32),
            pltpu.VMEM((WIN, 2 * width), BF16),
            pltpu.VMEM((streams, 2, HALF, width), BF16),
            pltpu.VMEM((streams, 2, HALF, width), BF16),
            pltpu.VMEM((streams, 2, HALF, width), BF16),
            pltpu.VMEM((streams, 2, HALF, width), BF16),
            pltpu.VMEM((streams * 2 * sections, HALF, columns), BF16),
            pltpu.VMEM((PASSED, HALF, columns), BF16),
            dma((4 + micro,)),
            dma((streams, 2)),
            dma,
            dma((streams, 2)),
            dma,
            dma,
            dma,
            dma,
            dma,
            dma((3,)),
            dma((3,)),
            dma((streams, 2)),
            dma,
            dma,
            dma,
            dma((PASSED,)),
            dma,
        ],
        compiler_params=pltpu.CompilerParams(
            collective_id=0, has_side_effects=True, vmem_limit_bytes=60 * 2**20
        ),
    )(inputs, norm_gain, w_qkv, w_out, w_head)
    decoded = decoded.reshape(micro, 2, 2, lat // 2, lon // 2, levels, columns)
    return decoded.transpose(0, 5, 1, 3, 2, 4, 6).reshape(micro, levels, lat, lon, columns)


def solution(mesh):
    placed = (
        P(None, None, None, "lon", None),
        P("section", None),
        P("section", None, None),
        P("section", None, None),
        P(None, "section"),
    )
    return jax.shard_map(
        per_device,
        mesh=mesh,
        in_specs=placed,
        out_specs=P(None, None, None, "lon", "section"),
        check_vma=False,
    )
```

```python
import functools

import jax
import jax.numpy as jnp
from jax import lax
from jax.experimental import pallas as pl
from jax.experimental.pallas import tpu as pltpu
from jax.sharding import PartitionSpec as P

MESH = pl.DeviceIdType.MESH
F32, BF16 = jnp.float32, jnp.bfloat16
HEADS = 8
PASSED = 4
HALF = 72
WIN = 2 * HALF
EPS = 1e-05
LAYERS = 8
SKIP = 5
LANES = 128


def dot(a, b):
    return jnp.dot(a, b, preferred_element_type=F32)


def dot_t(a, b):
    return lax.dot_general(a, b, (((1,), (1,)), ((), ())), preferred_element_type=F32)


def normalize(x, gain):
    mean = jnp.mean(x, axis=-1, keepdims=True)
    centred = x - mean
    spread = jnp.mean(centred * centred, axis=-1, keepdims=True)
    return (centred * lax.rsqrt(spread + EPS) * gain).astype(BF16)


def attend(query, kv, width):
    rows = query.shape[0]
    low = lax.broadcasted_iota(jnp.int32, (rows, LANES), 1) < LANES // 2
    weights = []
    for pair in range(width // LANES):
        cols = slice(pair * LANES, (pair + 1) * LANES)
        q = query[:, cols]
        both = jnp.concatenate([jnp.where(low, q, 0.0), jnp.where(low, 0.0, q)], 0).astype(BF16)
        scores = dot_t(both, kv[:, cols])
        top = jnp.max(scores, axis=-1, keepdims=True)
        weights.append(jnp.exp2(scores - top).astype(BF16))
    mixed = []
    for pair in range(width // LANES):
        values = kv[:, width + pair * LANES : width + (pair + 1) * LANES]
        summed = dot(weights[pair], jnp.concatenate([values, jnp.ones_like(values)], 1))
        summed = summed[:, :LANES] / summed[:, LANES:]
        mixed.append(jnp.where(low, summed[:rows], summed[rows:]))
    return jnp.concatenate(mixed, 1).astype(BF16)


def split(lon, lons):
    low = lax.rem(lon, 2)
    high = lon // (lons // 2)
    return high, lon - low - high * (lons // 2), low


def beside(high, middle, low, lons):
    flip = 1 - low
    usual = (high + flip - 2 * high * flip) * (lons // 2) + middle + low
    return usual, middle == lons // 2 - 2


def from_first(block, lons):
    _, middle, low = split(lax.rem(block + lons, lons), lons)
    return jnp.logical_or(low == 0, middle == lons // 2 - 2)


def holder(layer, block, lons):
    block = lax.rem(block + lons, lons)
    high, middle, low = split(block, lons)
    first = (0, block)
    usual, at_end = beside(high, middle, low, lons)
    second = (1, jnp.where(at_end, (1 - low) * (lons // 2) + middle + high, usual))
    later = (2 * (layer // 2) + low, block - low + lax.rem(layer, 2))
    return tuple(jnp.where(layer == 0, f, jnp.where(layer == 1, g, h)) for f, g, h in zip(first, second, later))


def role(sec, lon, lons):
    high, middle, low = split(lon, lons)
    side = lax.rem(sec, 2)
    layer = jnp.where(sec < 2, sec, sec - side + low)
    usual, at_end = beside(high, middle, low, lons)
    second = jnp.where(at_end, low * (lons // 2) + middle + 1 - high, usual)
    block = jnp.where(sec == 0, lon, jnp.where(sec == 1, second, lon - low + side))
    return layer, block


def kernel(micro, x_ref, gain_ref, wqkv_ref, wout_ref, whead_ref, out_ref,
           xin, gain, wqkv, wout, whead, xs, kv, arrived, skips, relayed, sent, outs, passed,
           load_sem, arrive_sem, send_sem, skip_sem, skipsend_sem, head_sem, headsend_sem, out_sem, outsend_sem,
           swap_sem, swapsend_sem, relay_sem, relaysend_sem, share_sem, sharesend_sem, pass_sem, passsend_sem):
    sections, lons = lax.axis_size("section"), lax.axis_size("lon")
    sec, lon = lax.axis_index("section"), lax.axis_index("lon")
    layer, mine = role(sec, lon, lons)
    odd = lax.rem(layer, 2)
    width = wout_ref.shape[-1]
    streams = 2 * micro
    last = LAYERS - 1
    core = lax.rem(lon, 2)
    side = lax.rem(sec, 2)
    swaps = jnp.logical_and(sec >= 2, side != core)
    keeps = jnp.logical_not(swaps)

    def target(half, to):
        return holder(to, mine + half - 1 + odd, lons)

    from_layer, from_block = role(sec - (sections - 2), lon, lons)

    def given(block):
        return [from_first(block + half - 1, lons) for half in range(2)]

    gives = [jnp.logical_and(layer == 0, g) for g in given(mine)]
    hands = [jnp.logical_and(sec == sections - 2, g) for g in given(from_block)]
    gives_input = jnp.logical_and(layer == 1, jnp.logical_not(from_first(mine, lons)))
    hands_input = jnp.logical_and(sec == sections - 1, jnp.logical_not(from_first(from_block, lons)))
    offers = jnp.logical_or(layer == 0, gives_input)
    relays = jnp.logical_or(sec == sections - 2, hands_input)
    straight = sec // 2 == 1

    partners = [(sec + 1 - 2 * side, lax.rem(lon + h * (lons // 2), lons) + 1 - 2 * core) for h in range(2)]

    loads = [
        pltpu.make_async_copy(gain_ref, gain, load_sem.at[0]),
        pltpu.make_async_copy(wqkv_ref.at[0], wqkv, load_sem.at[1]),
        pltpu.make_async_copy(wout_ref.at[0], wout, load_sem.at[2]),
    ]

    def load_x(m):
        return pltpu.make_async_copy(x_ref.at[m], xin.at[m], load_sem.at[4 + m])

    pl.when(layer == 0)(lambda: load_x(0).start())

    @pl.when(keeps)
    def _():
        loads[0].start()
        rows = width // 4
        for part in range(4):
            at = pl.ds(part * rows, rows)
            pltpu.make_async_copy(wqkv_ref.at[0, at], wqkv.at[at], load_sem.at[1]).start()
        loads[2].start()

    load_head = pltpu.make_async_copy(whead_ref, whead.at[side, sec // 2], load_sem.at[3])

    barrier = pltpu.get_barrier_semaphore()

    def greet(where):
        pl.semaphore_signal(barrier, inc=1, device_id=where, device_id_type=MESH)

    def source(behind, half):
        before = layer - behind
        return holder(before, mine - (half - 1 + lax.rem(before + LAYERS, 2)), lons)

    @pl.when(layer > 0)
    def _():
        for half in range(2):
            greet(source(1, half))

    @pl.when(jnp.logical_and(layer == SKIP, from_first(mine, lons)))
    def _():
        greet((sections - 2, mine))
        greet((sections - 2, lax.rem(mine + 1, lons)))

    @pl.when(jnp.logical_and(layer == SKIP, jnp.logical_not(from_first(mine, lons))))
    def _():
        greet((sections - 1, holder(jnp.int32(1), mine, lons)[1]))

    pl.when(layer > SKIP)(lambda: greet((sec - 4, lon)))
    pl.when(relays)(lambda: greet((sec - (sections - 2), lon)))
    passes = sec < sections - 2
    pl.when(passes)(lambda: greet((sec + 1 - 2 * side, lon)))

    @pl.when(swaps)
    def _():
        for where in partners:
            greet(where)

    for half in range(2):
        where = holder(jnp.int32(last), lon - half, lons)
        here = jnp.logical_and(where[0] == sec, where[1] == lon)
        pl.when(jnp.logical_not(here))(functools.partial(greet, where))

    @pl.when(layer == last)
    def _():
        for row in range(sections // 2 - 1):
            greet((2 * row + side, lon))
        greet((sec + 1 - 2 * side, lon))

    def place(stream):
        m, lat = stream // 2, lax.rem(stream, 2)
        pl.when(lat == 0)(lambda: load_x(m).wait())
        for half in range(2):
            for a in range(6):
                block = xin[m, lat * 6 + a, half * 6 : half * 6 + 6].astype(F32)
                at = half * HALF + a * 12
                xs[at : at + 12] = block.reshape(12, width)

    count = jnp.where(layer < last, 2, 2 * sections - 1) + jnp.where(swaps, 2, 0)
    for sends in (offers, straight, hands[0], hands[1], hands_input, passes, core == 1):
        count = count + jnp.where(sends, 1, 0)

    @pl.when(layer > 0)
    @jax.named_scope('greet')
    def _():
        pl.semaphore_wait(barrier, count)

    def swap_copy(half, piece):
        where = partners[half]
        rows = pl.ds(half * (width // 2), width // 2)
        src, dst = ((wqkv_ref.at[0, rows], wqkv.at[rows]), (wout_ref.at[0, rows], wout.at[rows]), (gain_ref, gain))[piece]
        return pltpu.make_async_remote_copy(
            src_ref=src, dst_ref=dst, send_sem=swapsend_sem.at[piece], recv_sem=swap_sem.at[piece],
            device_id=where, device_id_type=MESH)

    swap_list = ((0, 2), (0, 0), (1, 0), (0, 1), (1, 1))

    @pl.when(swaps)
    def _():
        for half, piece in swap_list:
            swap_copy(half, piece).start()

    def swap_wait(sems, piece):
        ref = (wqkv, wout, gain)[piece]
        pltpu.make_async_copy(ref, ref, sems.at[piece]).wait()

    def head_copy():
        mine_head = whead.at[side, sec // 2]
        return pltpu.make_async_remote_copy(
            src_ref=mine_head, dst_ref=mine_head, send_sem=headsend_sem, recv_sem=head_sem,
            device_id=(sections - 2 + side, lon), device_id_type=MESH)

    def share_copy():
        return pltpu.make_async_remote_copy(
            src_ref=whead.at[side], dst_ref=whead.at[side], send_sem=sharesend_sem, recv_sem=share_sem,
            device_id=(sec + 1 - 2 * side, lon), device_id_type=MESH)

    sends_head = jnp.logical_and(core == 1, sec < sections - 2)


    pl.when(layer == 0)(lambda: place(0))

    @pl.when(keeps)
    def _():
        for load in loads:
            load.wait()

    load_head.start()

    @pl.when(layer == 0)
    def _():
        for m in range(1, micro):
            load_x(m).start()

    def step_copy(stream, half):
        return pltpu.make_async_remote_copy(
            src_ref=sent.at[stream, half], dst_ref=arrived.at[stream, 1 - half],
            send_sem=send_sem, recv_sem=arrive_sem.at[stream, 1 - half],
            device_id=target(half, jnp.minimum(layer + 1, last)), device_id_type=MESH)

    def offer(ref, stream, half):
        return pltpu.make_async_remote_copy(
            src_ref=ref.at[stream, half], dst_ref=relayed.at[stream, half],
            send_sem=skipsend_sem, recv_sem=relay_sem.at[stream, half],
            device_id=(lax.rem(sec + sections - 2, sections), lon), device_id_type=MESH)

    def relay_out(stream, half, slot, block):
        return pltpu.make_async_remote_copy(
            src_ref=relayed.at[stream, half], dst_ref=skips.at[stream, slot],
            send_sem=relaysend_sem, recv_sem=skip_sem.at[stream, slot],
            device_id=holder(jnp.int32(SKIP), block, lons), device_id_type=MESH)

    def skip_copy(stream, half):
        return pltpu.make_async_remote_copy(
            src_ref=arrived.at[stream, half], dst_ref=skips.at[stream, half],
            send_sem=skipsend_sem, recv_sem=skip_sem.at[stream, half],
            device_id=(lax.rem(sec + 4, sections), lon), device_id_type=MESH)

    @jax.named_scope('relay')
    def relay(stream):
        for half in range(2):
            @pl.when(hands[half])
            def _():
                offer(sent, stream, half).wait_recv()
                relay_out(stream, half, 1 - half, from_block + half - 1).start()

        @pl.when(hands_input)
        def _():
            for half in range(2):
                offer(arrived, stream, half).wait_recv()
                relay_out(stream, half, half, from_block).start()

    def out_copy(stream, half, c):
        return pltpu.make_async_remote_copy(
            src_ref=outs.at[(stream * 2 + half) * sections + c], dst_ref=out_ref.at[stream, 1 - half],
            send_sem=outsend_sem, recv_sem=out_sem,
            device_id=(c, lax.rem(mine + half, lons)), device_id_type=MESH)

    def out_local(stream, half, c):
        return pltpu.make_async_copy(outs.at[(stream * 2 + half) * sections + c], out_ref.at[stream, 1 - half], out_sem)

    def stays(half, c):
        return jnp.logical_and(sec == c, lax.rem(mine + half, lons) == lon)

    def out_side(stream, to, rows=range(sections // 2)):
        for row in rows:
            c = 2 * row + to
            for half in range(2):
                if row < sections // 2 - 1:
                    out_copy(stream, half, c).start()
                else:
                    pl.when(jnp.logical_not(stays(half, c)))(lambda: out_copy(stream, half, c).start())
                    pl.when(stays(half, c))(lambda: out_local(stream, half, c).start())

    def pass_in(stream, half, row):
        c = 2 * row + 1 - side
        return pltpu.make_async_remote_copy(
            src_ref=outs.at[(stream * 2 + half) * sections + c], dst_ref=passed.at[stream],
            send_sem=outsend_sem, recv_sem=pass_sem.at[stream],
            device_id=(2 * row + side, lax.rem(mine + half, lons)), device_id_type=MESH)

    def pass_out(stream):
        slot = jnp.where(core == side, 1, 0)
        return pltpu.make_async_remote_copy(
            src_ref=passed.at[stream], dst_ref=out_ref.at[stream, slot], send_sem=passsend_sem, recv_sem=out_sem,
            device_id=(sec + 1 - 2 * side, lon), device_id_type=MESH)

    def send_head():
        load_head.wait()
        pl.when(sends_head)(lambda: head_copy().start())

    pl.when(layer > 0)(send_head)

    @pl.when(layer == last)
    @jax.named_scope('share')
    def _():
        others = whead.at[side, pl.ds(0, sections // 2 - 1)]
        pltpu.make_async_copy(others, others, head_sem).wait()
        share_copy().start()

    def relay_all():
        def one(stream, carry):
            relay(stream)
            return carry

        lax.fori_loop(0, streams, one, 0)

    pl.when(relays)(relay_all)

    def step(stream, carry):
        @pl.when(layer > 0)
        @jax.named_scope('arrive')
        def _():
            for half in range(2):
                step_copy(stream, 1 - half).wait_recv()

        pl.when(jnp.logical_and(layer == 0, stream > 0))(lambda: place(stream))

        @pl.when(gives_input)
        def _():
            for half in range(2):
                offer(arrived, stream, half).start()


        @pl.when(jnp.logical_and(layer > 0, layer < SKIP))
        def _():
            for half in range(2):
                xs[half * HALF : (half + 1) * HALF] = arrived[stream, half].astype(F32)

        @pl.when(layer >= SKIP)
        def _():
            for half in range(2):
                with jax.named_scope('skip'):
                    skip_copy(stream, half).wait_recv()
                joined = arrived[stream, half].astype(F32) + skips[stream, half].astype(F32)
                xs[half * HALF : (half + 1) * HALF] = joined.astype(BF16).astype(F32)

        def block(before_out):
            x = xs[...]
            normed = normalize(x, gain[...])
            query = dot(normed, wqkv[:, :width]) * ((width // HEADS) ** -0.5 * 1.4426950408889634)
            kv[...] = dot(normed, wqkv[:, width:]).astype(BF16)
            mixed = attend(query, kv, width)
            before_out()
            y = x + dot(mixed, wout[...])
            for half in range(2):
                sent[stream, half] = y[half * HALF : (half + 1) * HALF].astype(BF16)

        first_swapped = jnp.logical_and(swaps, stream == 0)
        in_a_hurry = jnp.logical_and(first_swapped, sec < 4)

        @pl.when(first_swapped)
        @jax.named_scope('swap')
        def _():
            swap_wait(swap_sem, 0)
            swap_wait(swap_sem, 2)
            pl.when(sec >= 4)(lambda: swap_wait(swap_sem, 1))

        @pl.when(in_a_hurry)
        def _():
            block(lambda: swap_wait(swap_sem, 1))

        @pl.when(jnp.logical_not(in_a_hurry))
        @jax.named_scope('block')
        def _():
            block(lambda: None)

        @pl.when(jnp.logical_and(layer == 0, stream == 0))
        @jax.named_scope('greet')
        def _():
            pl.semaphore_wait(barrier, count)

        @pl.when(layer < last)
        def _():
            for half in range(2):
                step_copy(stream, half).start()

        for half in range(2):
            pl.when(gives[half])(offer(sent, stream, half).start)

        pl.when(jnp.logical_and(layer == 0, stream == 0))(send_head)

        @pl.when(layer == last)
        @jax.named_scope('head')
        def _():
            @pl.when(stream == 0)
            @jax.named_scope('headwait')
            def _():
                share_copy().wait_recv()

            both = jnp.concatenate([sent[stream, 0].astype(F32), sent[stream, 1].astype(F32)], 0).astype(BF16)
            for pair in range(sections // 2):
                cols = jnp.concatenate([whead[0, pair], whead[1, pair]], 1)
                made = dot(both, cols)
                for part in range(2):
                    piece = made[:, part * LANES : (part + 1) * LANES]
                    for half in range(2):
                        rows = piece[half * HALF : (half + 1) * HALF]
                        outs[(stream * 2 + half) * sections + 2 * pair + part] = rows.astype(BF16)
            @pl.when(stream < PASSED)
            def _():
                for row in range(sections // 2 - 1):
                    for half in range(2):
                        pass_in(stream, half, row).start()
                out_side(stream, 1 - side, [sections // 2 - 1])

            pl.when(stream >= PASSED)(lambda: out_side(stream, 1 - side))
            out_side(stream, side)

        return carry

    lax.fori_loop(0, streams, step, 0)

    @pl.when(straight)
    def _():
        def send_skips(stream, carry):
            for half in range(2):
                skip_copy(stream, half).start()
            return carry

        lax.fori_loop(0, streams, send_skips, 0)

    @pl.when(passes)
    @jax.named_scope('pass')
    def _():
        def hand(stream, carry):
            pltpu.make_async_copy(passed.at[stream], passed.at[stream], pass_sem.at[stream]).wait()
            pass_out(stream).start()
            return carry

        lax.fori_loop(0, PASSED, hand, 0)

    with jax.named_scope('output'):
        pltpu.make_async_copy(out_ref, out_ref, out_sem).wait()

    @pl.when(layer < last)
    def _():
        pltpu.make_async_copy(sent, sent, send_sem).wait()

    def left(ref, sem):
        pltpu.make_async_copy(ref, ref, sem).wait()

    pl.when(passes)(lambda: left(passed, passsend_sem))
    def left_halves(ref, sem, which):
        one, both = jnp.logical_xor(*which), jnp.logical_and(*which)
        pl.when(one)(lambda: left(ref.at[pl.ds(0, streams // 2)], sem))
        pl.when(both)(lambda: left(ref, sem))

    left_halves(sent, skipsend_sem, gives)
    left_halves(relayed, relaysend_sem, hands)
    pl.when(jnp.logical_or(straight, gives_input))(lambda: left(arrived, skipsend_sem))
    pl.when(hands_input)(lambda: left(relayed, relaysend_sem))

    @pl.when(layer == last)
    def _():
        most = outs.at[pl.ds(0, streams * (2 * sections - 1))]
        pltpu.make_async_copy(most, most, outsend_sem).wait()

    pl.when(sends_head)(lambda: head_copy().wait_send())

    @pl.when(layer == last)
    def _():
        share_copy().wait_send()

    @pl.when(swaps)
    def _():
        for piece in range(3):
            swap_wait(swapsend_sem, piece)


def per_device(inputs, norm_gain, w_qkv, w_out, w_head):
    inputs = inputs.transpose(0, 2, 3, 1, 4)
    micro, lat, lon, levels, width = inputs.shape
    sections = lax.axis_size("section")
    columns = w_head.shape[1]
    streams = 2 * micro
    dma = pltpu.SemaphoreType.DMA
    hbm = pl.BlockSpec(memory_space=pl.ANY)
    decoded = pl.pallas_call(
        functools.partial(kernel, micro),
        out_shape=jax.ShapeDtypeStruct((streams, 2, HALF, columns), BF16),
        in_specs=[hbm] * 5,
        out_specs=hbm,
        scratch_shapes=[
            pltpu.VMEM(inputs.shape, BF16),
            pltpu.VMEM(norm_gain.shape, F32),
            pltpu.VMEM(w_qkv.shape[1:], BF16),
            pltpu.VMEM(w_out.shape[1:], BF16),
            pltpu.VMEM((2, sections // 2) + w_head.shape, BF16),
            pltpu.VMEM((WIN, width), F32),
            pltpu.VMEM((WIN, 2 * width), BF16),
            pltpu.VMEM((streams, 2, HALF, width), BF16),
            pltpu.VMEM((streams, 2, HALF, width), BF16),
            pltpu.VMEM((streams, 2, HALF, width), BF16),
            pltpu.VMEM((streams, 2, HALF, width), BF16),
            pltpu.VMEM((streams * 2 * sections, HALF, columns), BF16),
            pltpu.VMEM((PASSED, HALF, columns), BF16),
            dma((4 + micro,)),
            dma((streams, 2)),
            dma,
            dma((streams, 2)),
            dma,
            dma,
            dma,
            dma,
            dma,
            dma((3,)),
            dma((3,)),
            dma((streams, 2)),
            dma,
            dma,
            dma,
            dma((PASSED,)),
            dma,
        ],
        compiler_params=pltpu.CompilerParams(
            collective_id=0, has_side_effects=True, vmem_limit_bytes=60 * 2**20
        ),
    )(inputs, norm_gain, w_qkv, w_out, w_head)
    decoded = decoded.reshape(micro, 2, 2, lat // 2, lon // 2, levels, columns)
    return decoded.transpose(0, 5, 1, 3, 2, 4, 6).reshape(micro, levels, lat, lon, columns)


def solution(mesh):
    placed = (
        P(None, None, None, "lon", None),
        P("section", None),
        P("section", None, None),
        P("section", None, None),
        P(None, "section"),
    )
    return jax.shard_map(
        per_device,
        mesh=mesh,
        in_specs=placed,
        out_specs=P(None, None, None, "lon", "section"),
        check_vma=False,
    )
```

```python
import functools

import jax
import jax.numpy as jnp
from jax import lax
from jax.experimental import pallas as pl
from jax.experimental.pallas import tpu as pltpu
from jax.sharding import PartitionSpec as P

MESH = pl.DeviceIdType.MESH
F32, BF16 = jnp.float32, jnp.bfloat16
HEADS = 8
PASSED = 5
HALF = 72
WIN = 2 * HALF
EPS = 1e-05
LAYERS = 8
SKIP = 5
LANES = 128


def dot(a, b):
    return jnp.dot(a, b, preferred_element_type=F32)


def dot_t(a, b):
    return lax.dot_general(a, b, (((1,), (1,)), ((), ())), preferred_element_type=F32)


def normalize(x, gain):
    mean = jnp.mean(x, axis=-1, keepdims=True)
    centred = x - mean
    spread = jnp.mean(centred * centred, axis=-1, keepdims=True)
    return (centred * lax.rsqrt(spread + EPS) * gain).astype(BF16)


def attend(query, kv, width):
    rows = query.shape[0]
    low = lax.broadcasted_iota(jnp.int32, (rows, LANES), 1) < LANES // 2
    weights = []
    for pair in range(width // LANES):
        cols = slice(pair * LANES, (pair + 1) * LANES)
        q = query[:, cols]
        both = jnp.concatenate([jnp.where(low, q, 0.0), jnp.where(low, 0.0, q)], 0).astype(BF16)
        scores = dot_t(both, kv[:, cols])
        top = jnp.max(scores, axis=-1, keepdims=True)
        weights.append(jnp.exp2(scores - top).astype(BF16))
    mixed = []
    for pair in range(width // LANES):
        values = kv[:, width + pair * LANES : width + (pair + 1) * LANES]
        summed = dot(weights[pair], jnp.concatenate([values, jnp.ones_like(values)], 1))
        summed = summed[:, :LANES] / summed[:, LANES:]
        mixed.append(jnp.where(low, summed[:rows], summed[rows:]))
    return jnp.concatenate(mixed, 1).astype(BF16)


def split(lon, lons):
    low = lax.rem(lon, 2)
    high = lon // (lons // 2)
    return high, lon - low - high * (lons // 2), low


def beside(high, middle, low, lons):
    flip = 1 - low
    usual = (high + flip - 2 * high * flip) * (lons // 2) + middle + low
    return usual, middle == lons // 2 - 2


def from_first(block, lons):
    _, middle, low = split(lax.rem(block + lons, lons), lons)
    return jnp.logical_or(low == 0, middle == lons // 2 - 2)


def holder(layer, block, lons):
    block = lax.rem(block + lons, lons)
    high, middle, low = split(block, lons)
    first = (0, block)
    usual, at_end = beside(high, middle, low, lons)
    second = (1, jnp.where(at_end, (1 - low) * (lons // 2) + middle + high, usual))
    later = (2 * (layer // 2) + low, block - low + lax.rem(layer, 2))
    return tuple(jnp.where(layer == 0, f, jnp.where(layer == 1, g, h)) for f, g, h in zip(first, second, later))


def role(sec, lon, lons):
    high, middle, low = split(lon, lons)
    side = lax.rem(sec, 2)
    layer = jnp.where(sec < 2, sec, sec - side + low)
    usual, at_end = beside(high, middle, low, lons)
    second = jnp.where(at_end, low * (lons // 2) + middle + 1 - high, usual)
    block = jnp.where(sec == 0, lon, jnp.where(sec == 1, second, lon - low + side))
    return layer, block


def kernel(micro, x_ref, gain_ref, wqkv_ref, wout_ref, whead_ref, out_ref,
           xin, gain, wqkv, wout, whead, xs, kv, arrived, skips, relayed, sent, outs, passed,
           load_sem, arrive_sem, send_sem, skip_sem, skipsend_sem, head_sem, headsend_sem, out_sem, outsend_sem,
           swap_sem, swapsend_sem, relay_sem, relaysend_sem, share_sem, sharesend_sem, pass_sem, passsend_sem):
    sections, lons = lax.axis_size("section"), lax.axis_size("lon")
    sec, lon = lax.axis_index("section"), lax.axis_index("lon")
    layer, mine = role(sec, lon, lons)
    odd = lax.rem(layer, 2)
    width = wout_ref.shape[-1]
    streams = 2 * micro
    last = LAYERS - 1
    core = lax.rem(lon, 2)
    side = lax.rem(sec, 2)
    swaps = jnp.logical_and(sec >= 2, side != core)
    keeps = jnp.logical_not(swaps)

    def target(half, to):
        return holder(to, mine + half - 1 + odd, lons)

    from_layer, from_block = role(sec - (sections - 2), lon, lons)

    def given(block):
        return [from_first(block + half - 1, lons) for half in range(2)]

    gives = [jnp.logical_and(layer == 0, g) for g in given(mine)]
    hands = [jnp.logical_and(sec == sections - 2, g) for g in given(from_block)]
    gives_input = jnp.logical_and(layer == 1, jnp.logical_not(from_first(mine, lons)))
    hands_input = jnp.logical_and(sec == sections - 1, jnp.logical_not(from_first(from_block, lons)))
    offers = jnp.logical_or(layer == 0, gives_input)
    relays = jnp.logical_or(sec == sections - 2, hands_input)
    straight = sec // 2 == 1

    partners = [(sec + 1 - 2 * side, lax.rem(lon + h * (lons // 2), lons) + 1 - 2 * core) for h in range(2)]

    loads = [
        pltpu.make_async_copy(gain_ref, gain, load_sem.at[0]),
        pltpu.make_async_copy(wqkv_ref.at[0], wqkv, load_sem.at[1]),
        pltpu.make_async_copy(wout_ref.at[0], wout, load_sem.at[2]),
    ]

    def load_x(m):
        return pltpu.make_async_copy(x_ref.at[m], xin.at[m], load_sem.at[4 + m])

    pl.when(layer == 0)(lambda: load_x(0).start())

    @pl.when(keeps)
    def _():
        loads[0].start()
        rows = width // 4
        for part in range(4):
            at = pl.ds(part * rows, rows)
            pltpu.make_async_copy(wqkv_ref.at[0, at], wqkv.at[at], load_sem.at[1]).start()
        loads[2].start()

    load_head = pltpu.make_async_copy(whead_ref, whead.at[side, sec // 2], load_sem.at[3])

    barrier = pltpu.get_barrier_semaphore()

    def greet(where):
        pl.semaphore_signal(barrier, inc=1, device_id=where, device_id_type=MESH)

    def source(behind, half):
        before = layer - behind
        return holder(before, mine - (half - 1 + lax.rem(before + LAYERS, 2)), lons)

    @pl.when(layer > 0)
    def _():
        for half in range(2):
            greet(source(1, half))

    @pl.when(jnp.logical_and(layer == SKIP, from_first(mine, lons)))
    def _():
        greet((sections - 2, mine))
        greet((sections - 2, lax.rem(mine + 1, lons)))

    @pl.when(jnp.logical_and(layer == SKIP, jnp.logical_not(from_first(mine, lons))))
    def _():
        greet((sections - 1, holder(jnp.int32(1), mine, lons)[1]))

    pl.when(layer > SKIP)(lambda: greet((sec - 4, lon)))
    pl.when(relays)(lambda: greet((sec - (sections - 2), lon)))
    passes = sec < sections - 2
    pl.when(passes)(lambda: greet((sec + 1 - 2 * side, lon)))

    @pl.when(swaps)
    def _():
        for where in partners:
            greet(where)

    for half in range(2):
        where = holder(jnp.int32(last), lon - half, lons)
        here = jnp.logical_and(where[0] == sec, where[1] == lon)
        pl.when(jnp.logical_not(here))(functools.partial(greet, where))

    @pl.when(layer == last)
    def _():
        for row in range(sections // 2 - 1):
            greet((2 * row + side, lon))
        greet((sec + 1 - 2 * side, lon))

    def place(stream):
        m, lat = stream // 2, lax.rem(stream, 2)
        pl.when(lat == 0)(lambda: load_x(m).wait())
        for half in range(2):
            for a in range(6):
                block = xin[m, lat * 6 + a, half * 6 : half * 6 + 6].astype(F32)
                at = half * HALF + a * 12
                xs[at : at + 12] = block.reshape(12, width)

    count = jnp.where(layer < last, 2, 2 * sections - 1) + jnp.where(swaps, 2, 0)
    for sends in (offers, straight, hands[0], hands[1], hands_input, passes, core == 1):
        count = count + jnp.where(sends, 1, 0)

    @pl.when(layer > 0)
    @jax.named_scope('greet')
    def _():
        pl.semaphore_wait(barrier, count)

    def swap_copy(half, piece):
        where = partners[half]
        rows = pl.ds(half * (width // 2), width // 2)
        src, dst = ((wqkv_ref.at[0, rows], wqkv.at[rows]), (wout_ref.at[0, rows], wout.at[rows]), (gain_ref, gain))[piece]
        return pltpu.make_async_remote_copy(
            src_ref=src, dst_ref=dst, send_sem=swapsend_sem.at[piece], recv_sem=swap_sem.at[piece],
            device_id=where, device_id_type=MESH)

    swap_list = ((0, 2), (0, 0), (1, 0), (0, 1), (1, 1))

    @pl.when(swaps)
    def _():
        for half, piece in swap_list:
            swap_copy(half, piece).start()

    def swap_wait(sems, piece):
        ref = (wqkv, wout, gain)[piece]
        pltpu.make_async_copy(ref, ref, sems.at[piece]).wait()

    def head_copy():
        mine_head = whead.at[side, sec // 2]
        return pltpu.make_async_remote_copy(
            src_ref=mine_head, dst_ref=mine_head, send_sem=headsend_sem, recv_sem=head_sem,
            device_id=(sections - 2 + side, lon), device_id_type=MESH)

    def share_copy():
        return pltpu.make_async_remote_copy(
            src_ref=whead.at[side], dst_ref=whead.at[side], send_sem=sharesend_sem, recv_sem=share_sem,
            device_id=(sec + 1 - 2 * side, lon), device_id_type=MESH)

    sends_head = jnp.logical_and(core == 1, sec < sections - 2)


    pl.when(layer == 0)(lambda: place(0))

    @pl.when(keeps)
    def _():
        for load in loads:
            load.wait()

    load_head.start()

    @pl.when(layer == 0)
    def _():
        for m in range(1, micro):
            load_x(m).start()

    def step_copy(stream, half):
        return pltpu.make_async_remote_copy(
            src_ref=sent.at[stream, half], dst_ref=arrived.at[stream, 1 - half],
            send_sem=send_sem, recv_sem=arrive_sem.at[stream, 1 - half],
            device_id=target(half, jnp.minimum(layer + 1, last)), device_id_type=MESH)

    def offer(ref, stream, half):
        return pltpu.make_async_remote_copy(
            src_ref=ref.at[stream, half], dst_ref=relayed.at[stream, half],
            send_sem=skipsend_sem, recv_sem=relay_sem.at[stream, half],
            device_id=(lax.rem(sec + sections - 2, sections), lon), device_id_type=MESH)

    def relay_out(stream, half, slot, block):
        return pltpu.make_async_remote_copy(
            src_ref=relayed.at[stream, half], dst_ref=skips.at[stream, slot],
            send_sem=relaysend_sem, recv_sem=skip_sem.at[stream, slot],
            device_id=holder(jnp.int32(SKIP), block, lons), device_id_type=MESH)

    def skip_copy(stream, half):
        return pltpu.make_async_remote_copy(
            src_ref=arrived.at[stream, half], dst_ref=skips.at[stream, half],
            send_sem=skipsend_sem, recv_sem=skip_sem.at[stream, half],
            device_id=(lax.rem(sec + 4, sections), lon), device_id_type=MESH)

    @jax.named_scope('relay')
    def relay(stream):
        for half in range(2):
            @pl.when(hands[half])
            def _():
                offer(sent, stream, half).wait_recv()
                relay_out(stream, half, 1 - half, from_block + half - 1).start()

        @pl.when(hands_input)
        def _():
            for half in range(2):
                offer(arrived, stream, half).wait_recv()
                relay_out(stream, half, half, from_block).start()

    def out_copy(stream, half, c):
        return pltpu.make_async_remote_copy(
            src_ref=outs.at[(stream * 2 + half) * sections + c], dst_ref=out_ref.at[stream, 1 - half],
            send_sem=outsend_sem, recv_sem=out_sem,
            device_id=(c, lax.rem(mine + half, lons)), device_id_type=MESH)

    def out_local(stream, half, c):
        return pltpu.make_async_copy(outs.at[(stream * 2 + half) * sections + c], out_ref.at[stream, 1 - half], out_sem)

    def stays(half, c):
        return jnp.logical_and(sec == c, lax.rem(mine + half, lons) == lon)

    def out_side(stream, to, rows=range(sections // 2)):
        for row in rows:
            c = 2 * row + to
            for half in range(2):
                if row < sections // 2 - 1:
                    out_copy(stream, half, c).start()
                else:
                    pl.when(jnp.logical_not(stays(half, c)))(lambda: out_copy(stream, half, c).start())
                    pl.when(stays(half, c))(lambda: out_local(stream, half, c).start())

    def pass_in(stream, half, row):
        c = 2 * row + 1 - side
        return pltpu.make_async_remote_copy(
            src_ref=outs.at[(stream * 2 + half) * sections + c], dst_ref=passed.at[stream],
            send_sem=outsend_sem, recv_sem=pass_sem.at[stream],
            device_id=(2 * row + side, lax.rem(mine + half, lons)), device_id_type=MESH)

    def pass_out(stream):
        slot = jnp.where(core == side, 1, 0)
        return pltpu.make_async_remote_copy(
            src_ref=passed.at[stream], dst_ref=out_ref.at[stream, slot], send_sem=passsend_sem, recv_sem=out_sem,
            device_id=(sec + 1 - 2 * side, lon), device_id_type=MESH)

    def send_head():
        load_head.wait()
        pl.when(sends_head)(lambda: head_copy().start())

    pl.when(layer > 0)(send_head)

    @pl.when(layer == last)
    @jax.named_scope('share')
    def _():
        others = whead.at[side, pl.ds(0, sections // 2 - 1)]
        pltpu.make_async_copy(others, others, head_sem).wait()
        share_copy().start()

    def relay_all():
        def one(stream, carry):
            relay(stream)
            return carry

        lax.fori_loop(0, streams, one, 0)

    pl.when(relays)(relay_all)

    def step(stream, carry):
        @pl.when(layer > 0)
        @jax.named_scope('arrive')
        def _():
            for half in range(2):
                step_copy(stream, 1 - half).wait_recv()

        pl.when(jnp.logical_and(layer == 0, stream > 0))(lambda: place(stream))

        @pl.when(gives_input)
        def _():
            for half in range(2):
                offer(arrived, stream, half).start()


        @pl.when(jnp.logical_and(layer > 0, layer < SKIP))
        def _():
            for half in range(2):
                xs[half * HALF : (half + 1) * HALF] = arrived[stream, half].astype(F32)

        @pl.when(layer >= SKIP)
        def _():
            for half in range(2):
                with jax.named_scope('skip'):
                    skip_copy(stream, half).wait_recv()
                joined = arrived[stream, half].astype(F32) + skips[stream, half].astype(F32)
                xs[half * HALF : (half + 1) * HALF] = joined.astype(BF16).astype(F32)

        def block(before_out):
            x = xs[...]
            normed = normalize(x, gain[...])
            query = dot(normed, wqkv[:, :width]) * ((width // HEADS) ** -0.5 * 1.4426950408889634)
            kv[...] = dot(normed, wqkv[:, width:]).astype(BF16)
            mixed = attend(query, kv, width)
            before_out()
            y = x + dot(mixed, wout[...])
            for half in range(2):
                sent[stream, half] = y[half * HALF : (half + 1) * HALF].astype(BF16)

        first_swapped = jnp.logical_and(swaps, stream == 0)
        in_a_hurry = jnp.logical_and(first_swapped, sec < 4)

        @pl.when(first_swapped)
        @jax.named_scope('swap')
        def _():
            swap_wait(swap_sem, 0)
            swap_wait(swap_sem, 2)
            pl.when(sec >= 4)(lambda: swap_wait(swap_sem, 1))

        @pl.when(in_a_hurry)
        def _():
            block(lambda: swap_wait(swap_sem, 1))

        @pl.when(jnp.logical_not(in_a_hurry))
        @jax.named_scope('block')
        def _():
            block(lambda: None)

        @pl.when(jnp.logical_and(layer == 0, stream == 0))
        @jax.named_scope('greet')
        def _():
            pl.semaphore_wait(barrier, count)

        @pl.when(layer < last)
        def _():
            for half in range(2):
                step_copy(stream, half).start()

        for half in range(2):
            pl.when(gives[half])(offer(sent, stream, half).start)

        pl.when(jnp.logical_and(layer == 0, stream == 0))(send_head)

        @pl.when(layer == last)
        @jax.named_scope('head')
        def _():
            @pl.when(stream == 0)
            @jax.named_scope('headwait')
            def _():
                share_copy().wait_recv()

            both = jnp.concatenate([sent[stream, 0].astype(F32), sent[stream, 1].astype(F32)], 0).astype(BF16)
            for pair in range(sections // 2):
                cols = jnp.concatenate([whead[0, pair], whead[1, pair]], 1)
                made = dot(both, cols)
                for part in range(2):
                    piece = made[:, part * LANES : (part + 1) * LANES]
                    for half in range(2):
                        rows = piece[half * HALF : (half + 1) * HALF]
                        outs[(stream * 2 + half) * sections + 2 * pair + part] = rows.astype(BF16)
            @pl.when(stream < PASSED)
            def _():
                for row in range(sections // 2 - 1):
                    for half in range(2):
                        pass_in(stream, half, row).start()
                out_side(stream, 1 - side, [sections // 2 - 1])

            pl.when(stream >= PASSED)(lambda: out_side(stream, 1 - side))
            out_side(stream, side)

        return carry

    lax.fori_loop(0, streams, step, 0)

    @pl.when(straight)
    def _():
        def send_skips(stream, carry):
            for half in range(2):
                skip_copy(stream, half).start()
            return carry

        lax.fori_loop(0, streams, send_skips, 0)

    @pl.when(passes)
    @jax.named_scope('pass')
    def _():
        def hand(stream, carry):
            pltpu.make_async_copy(passed.at[stream], passed.at[stream], pass_sem.at[stream]).wait()
            pass_out(stream).start()
            return carry

        lax.fori_loop(0, PASSED, hand, 0)

    with jax.named_scope('output'):
        pltpu.make_async_copy(out_ref, out_ref, out_sem).wait()

    @pl.when(layer < last)
    def _():
        pltpu.make_async_copy(sent, sent, send_sem).wait()

    def left(ref, sem):
        pltpu.make_async_copy(ref, ref, sem).wait()

    pl.when(passes)(lambda: left(passed, passsend_sem))
    def left_halves(ref, sem, which):
        one, both = jnp.logical_xor(*which), jnp.logical_and(*which)
        pl.when(one)(lambda: left(ref.at[pl.ds(0, streams // 2)], sem))
        pl.when(both)(lambda: left(ref, sem))

    left_halves(sent, skipsend_sem, gives)
    left_halves(relayed, relaysend_sem, hands)
    pl.when(jnp.logical_or(straight, gives_input))(lambda: left(arrived, skipsend_sem))
    pl.when(hands_input)(lambda: left(relayed, relaysend_sem))

    @pl.when(layer == last)
    def _():
        most = outs.at[pl.ds(0, streams * (2 * sections - 1))]
        pltpu.make_async_copy(most, most, outsend_sem).wait()

    pl.when(sends_head)(lambda: head_copy().wait_send())

    @pl.when(layer == last)
    def _():
        share_copy().wait_send()

    @pl.when(swaps)
    def _():
        for piece in range(3):
            swap_wait(swapsend_sem, piece)


def per_device(inputs, norm_gain, w_qkv, w_out, w_head):
    inputs = inputs.transpose(0, 2, 3, 1, 4)
    micro, lat, lon, levels, width = inputs.shape
    sections = lax.axis_size("section")
    columns = w_head.shape[1]
    streams = 2 * micro
    dma = pltpu.SemaphoreType.DMA
    hbm = pl.BlockSpec(memory_space=pl.ANY)
    decoded = pl.pallas_call(
        functools.partial(kernel, micro),
        out_shape=jax.ShapeDtypeStruct((streams, 2, HALF, columns), BF16),
        in_specs=[hbm] * 5,
        out_specs=hbm,
        scratch_shapes=[
            pltpu.VMEM(inputs.shape, BF16),
            pltpu.VMEM(norm_gain.shape, F32),
            pltpu.VMEM(w_qkv.shape[1:], BF16),
            pltpu.VMEM(w_out.shape[1:], BF16),
            pltpu.VMEM((2, sections // 2) + w_head.shape, BF16),
            pltpu.VMEM((WIN, width), F32),
            pltpu.VMEM((WIN, 2 * width), BF16),
            pltpu.VMEM((streams, 2, HALF, width), BF16),
            pltpu.VMEM((streams, 2, HALF, width), BF16),
            pltpu.VMEM((streams, 2, HALF, width), BF16),
            pltpu.VMEM((streams, 2, HALF, width), BF16),
            pltpu.VMEM((streams * 2 * sections, HALF, columns), BF16),
            pltpu.VMEM((PASSED, HALF, columns), BF16),
            dma((4 + micro,)),
            dma((streams, 2)),
            dma,
            dma((streams, 2)),
            dma,
            dma,
            dma,
            dma,
            dma,
            dma((3,)),
            dma((3,)),
            dma((streams, 2)),
            dma,
            dma,
            dma,
            dma((PASSED,)),
            dma,
        ],
        compiler_params=pltpu.CompilerParams(
            collective_id=0, has_side_effects=True, vmem_limit_bytes=60 * 2**20
        ),
    )(inputs, norm_gain, w_qkv, w_out, w_head)
    decoded = decoded.reshape(micro, 2, 2, lat // 2, lon // 2, levels, columns)
    return decoded.transpose(0, 5, 1, 3, 2, 4, 6).reshape(micro, levels, lat, lon, columns)


def solution(mesh):
    placed = (
        P(None, None, None, "lon", None),
        P("section", None),
        P("section", None, None),
        P("section", None, None),
        P(None, "section"),
    )
    return jax.shard_map(
        per_device,
        mesh=mesh,
        in_specs=placed,
        out_specs=P(None, None, None, "lon", "section"),
        check_vma=False,
    )
```
